32 devices in a mesh: wide: 8 (over z, x), narrow: 4 (over y, core).
Axes of the slice: x: 2, y: 2, z: 4, core: 2. Of those that a mesh axis runs over, the one named last changes fastest.
Arguments:
- tokens: bfloat16 [8192, 2048], P(('wide', 'narrow')), may hold values from -6 to 6
- documents: int32 [8, 1024], P('wide'), may hold values from 0 to 3, never falling along the last dimension, each value on 1 to 512 neighbouring positions
- head_level: int32 [8192], P(('wide', 'narrow')), may hold values from 0 to 3
- width_level: int32 [8192], P(('wide', 'narrow')), may hold values from 0 to 3
- mixer_gain: float32 [2048], replicated, may hold values from 0.5 to 1.5
- mixer_bias: float32 [2048], replicated, may hold values from -1.5 to 1.5
- input_weight: bfloat16 [2048, 6144], P(('wide', 'narrow')), may hold values from -0.125 to 0.125
- output_weight: bfloat16 [2048, 2048], P(('wide', 'narrow')), may hold values from -0.75 to 0.75
- mixer_router: float32 [2048, 4], replicated, may hold values from -0.125 to 0.125
- feed_gain: float32 [2048], replicated, may hold values from 0.5 to 1.5
- feed_bias: float32 [2048], replicated, may hold values from -1.5 to 1.5
- up_weight: bfloat16 [2048, 8192], P(('wide', 'narrow')), may hold values from -0.125 to 0.125
- down_weight: bfloat16 [8192, 2048], P(('wide', 'narrow')), may hold values from -0.0625 to 0.0625
- feed_router: float32 [2048, 4], replicated, may hold values from -0.125 to 0.125
- cotangent: bfloat16 [8192, 2048], P(('wide', 'narrow')), may hold values from -6 to 6
Outputs:
- outputs: bfloat16 [8192, 2048], P(('wide', 'narrow'))
- grad_tokens: float32 [8192, 2048], P(('wide', 'narrow'))
- grad_mixer_gain: float32 [2048], replicated
- grad_mixer_bias: float32 [2048], replicated
- grad_input_weight: float32 [2048, 6144], P(('wide', 'narrow'))
- grad_output_weight: float32 [2048, 2048], P(('wide', 'narrow'))
- grad_mixer_router: float32 [2048, 4], replicated
- grad_feed_gain: float32 [2048], replicated
- grad_feed_bias: float32 [2048], replicated
- grad_up_weight: float32 [2048, 8192], P(('wide', 'narrow'))
- grad_down_weight: float32 [8192, 2048], P(('wide', 'narrow'))
- grad_feed_router: float32 [2048, 4], replicated
- usage_counts: float32 [2, 4], replicated
The draws below stay inside these ranges and needn't reach their ends.
Inputs may be any that keep to these rules, and one draw needn't show every extreme that they name: `documents`: along each sequence the document id never falls; a document has at most 512 positions, and one has exactly that many.
All inputs are finite; a program needn't handle non-finite values.
Results may differ from the reference program's by a relative error of at most 0.013.
Values may be sent and summed in bfloat16 or wider, within the bound.
No kernel may reach another device: no remote copies, remote signals or barrier semaphores. Data moves between devices by JAX's collectives and lax.ppermute only.
A program may use at most 448 MiB of HBM per device.

```python
import math
import jax
import jax.numpy as jnp
import numpy as np
from jax import lax

D = 2048
H = 16
HD = 128
FF = 8192
OPTIONS = 4
SEQ = 1024
NSEQ = 8
TOKENS = 8192


def place_ends(drawn, rng, least, top_value):
    dims = drawn.shape
    place = [jax.random.randint(jax.random.fold_in(rng, axis), (), 0, dims[axis]) for axis in range(len(dims))]
    drawn = drawn.at[tuple(place)].set(least)
    longest = dims.index(max(dims))
    place[longest] = (place[longest] + 1) % dims[longest]
    return drawn.at[tuple(place)].set(top_value)


def steps_of(rng, extent, cuts, low, largest):
    def one(position, blocks):
        steps = jax.random.uniform(jax.random.fold_in(jax.random.fold_in(rng, 6), position), (blocks,), jnp.float32, low / len(cuts), largest / len(cuts))
        return jnp.repeat(jnp.exp(steps), extent[position] // blocks).reshape((-1,) + (1,) * (len(extent) - position - 1))

    level = one(*cuts[0])
    for cut in cuts[1:]:
        level = level * one(*cut)
    return level


def length_profile(count, total, most, lean):
    portions = [(1 << 20) // math.isqrt(rank ** lean) + 1 for rank in range(2, count + 1)]
    rest, holding = total - most - (count - 1), [1] * (count - 1)
    while rest > 0:
        movable = [i for i in range(count - 1) if holding[i] < most]
        mass, left = sum([portions[i] for i in movable]), rest
        for i in movable:
            extra = min(most - holding[i], max(1, left * portions[i] // mass), rest)
            holding[i] = holding[i] + extra
            rest = rest - extra
    return np.array([most] + holding)


def ragged(rng, number_of, total, most, slope):
    if number_of == 2:
        one = jax.random.randint(rng, (), max(1, total - most), min(most, total - 1) + 1)
        return jnp.stack([one, total - one])
    tallies = jnp.asarray(length_profile(number_of, total, most, slope), jnp.int32)
    couples = (number_of - 1) // 2
    source_of, receiver = tallies[1:1 + 2 * couples:2], tallies[2:2 + 2 * couples:2]
    slack = jnp.minimum(source_of - 1, most - receiver)
    passed = jax.random.randint(jax.random.fold_in(rng, 1), (couples,), 0, 1 << 20) % (slack + 1)
    tallies = tallies.at[1:1 + 2 * couples:2].set(source_of - passed).at[2:2 + 2 * couples:2].set(receiver + passed)
    return tallies[jax.random.permutation(jax.random.fold_in(rng, 2), number_of)]


def gaussian(own_key, shape, deviation, limit, shards=(), dtype=jnp.bfloat16):
    entries = jax.random.normal(own_key, shape, jnp.float32) * deviation
    if len(shards) > 0:
        entries = steps_of(own_key, shape, shards, -0.22, 0.18) * entries
    return jnp.clip(entries, min=-limit, max=limit).astype(dtype)


def setup_inputs(seed: int = 0) -> dict:
    splits = jax.random.split(jax.random.key(seed), 16)
    return {
        "tokens": gaussian(splits[0], (TOKENS, D), 1.0, 6.0, ((0, 32),)),
        "documents": jax.vmap(lambda own: jnp.searchsorted(jnp.cumsum(ragged(own, 4, SEQ, SEQ // 2, 1)), jnp.arange(SEQ), side="right"))(jax.random.split(splits[1], NSEQ)).reshape((NSEQ, SEQ)).astype(jnp.int32),
        "head_level": place_ends(jax.random.randint(splits[2], (TOKENS,), 0, OPTIONS), jax.random.fold_in(splits[2], 1), 0, OPTIONS - 1).astype(jnp.int32),
        "width_level": place_ends(jax.random.randint(splits[3], (TOKENS,), 0, OPTIONS), jax.random.fold_in(splits[3], 1), 0, OPTIONS - 1).astype(jnp.int32),
        "mixer_gain": jnp.clip(1.0 + 0.1 * jax.random.normal(splits[4], (D,), jnp.float32), 0.5, 1.5),
        "mixer_bias": gaussian(splits[5], (D,), 0.3, 1.5, (), jnp.float32),
        "input_weight": gaussian(splits[6], (D, 3 * D), D ** -0.5, 0.125, ((0, 32),)),
        "output_weight": gaussian(splits[7], (D, D), (D // 32) ** -0.5, 0.75, ((0, 32),)),
        "mixer_router": gaussian(splits[8], (D, OPTIONS), D ** -0.5, 0.125, (), jnp.float32),
        "feed_gain": jnp.clip(1.0 + 0.1 * jax.random.normal(splits[9], (D,), jnp.float32), 0.5, 1.5),
        "feed_bias": gaussian(splits[10], (D,), 0.3, 1.5, (), jnp.float32),
        "up_weight": gaussian(splits[11], (D, FF), D ** -0.5, 0.125, ((0, 32),)),
        "down_weight": gaussian(splits[12], (FF, D), FF ** -0.5, 0.0625, ((0, 32),)),
        "feed_router": gaussian(splits[13], (D, OPTIONS), D ** -0.5, 0.125, (), jnp.float32),
        "cotangent": gaussian(splits[14], (TOKENS, D), 1.0, 6.0, ((0, 32),)),
    }


@jax.custom_vjp
def low(v):
    return lax.optimization_barrier(v.astype(jnp.bfloat16)).astype(jnp.float32)

@jax.custom_vjp
def low_back(v):
    return v

def low_keep(v):
    return (low(v), None)

def low_pass(kept, grad):
    return (grad,)

def back_keep(v):
    return (v, None)

def back_low(kept, grad):
    return (low(grad),)
low.defvjp(low_keep, low_pass)
low_back.defvjp(back_keep, back_low)
highest = lax.Precision.HIGHEST
epsilon = 1e-05
masked_score = -1e+30

def normalize(values, gain_vec, shift_vec):
    centre = values - lax.optimization_barrier(jnp.mean(values, axis=1, keepdims=True))
    inv_scale = lax.rsqrt(lax.optimization_barrier(jnp.mean(centre * centre, axis=1, keepdims=True)) + epsilon)
    return centre * inv_scale * gain_vec + shift_vec

def route_gate(hidden, router, picked):
    logits = jnp.dot(hidden, router, precision=highest)
    shifted = jnp.exp(logits - lax.optimization_barrier(jnp.max(logits, axis=1, keepdims=True)))
    prob_rows = shifted / lax.optimization_barrier(jnp.sum(shifted, axis=1, keepdims=True))
    chosen = (jnp.arange(OPTIONS)[None, :] == picked[:, None]).astype(jnp.float32)
    return OPTIONS * lax.optimization_barrier(jnp.sum(prob_rows * chosen, axis=1))

def rope_tables(positions):
    half_width = HD // 2
    exponent = jnp.arange(half_width).astype(jnp.float32) * (-2.0 / HD)
    frequency = jnp.power(10000.0, exponent)
    angles = positions[:, None] * frequency[None, :]
    return (jnp.cos(angles), jnp.sin(angles))

def rotate(values, cos_table, sin_table):
    row_count = values.shape[0]
    by_heads = values.reshape(row_count, values.shape[1] // HD, HD)
    half_width = HD // 2
    lower_part = by_heads[:, :, :half_width]
    upper_part = by_heads[:, :, half_width:]
    cos_rows = cos_table[:, None, :]
    sin_rows = sin_table[:, None, :]
    rotated = jnp.concatenate([lower_part * cos_rows - upper_part * sin_rows, upper_part * cos_rows + lower_part * sin_rows], axis=2)
    return rotated.reshape(row_count, values.shape[1])

def sequence_layer(weights, pieces):
    mixer_gain, mixer_bias, input_weight, output_weight, mixer_router, feed_gain, feed_bias, up_weight, down_weight, feed_router = weights
    token_rows, document_row, head_row, width_row = pieces
    positions = jnp.arange(SEQ).astype(jnp.float32)
    cos_table, sin_table = rope_tables(positions)
    mixer_hidden = normalize(token_rows, mixer_gain, mixer_bias)
    mixer_gate = route_gate(mixer_hidden, mixer_router, head_row)
    projected = low_back(jnp.dot(low(mixer_hidden), input_weight, precision=highest))
    queries = low(rotate(projected[:, :D], cos_table, sin_table))
    keys_rot = low(rotate(projected[:, D:2 * D], cos_table, sin_table))
    values_low = low(projected[:, 2 * D:])
    query_heads = queries.reshape(SEQ, H, HD)
    key_heads = keys_rot.reshape(SEQ, H, HD)
    value_heads = values_low.reshape(SEQ, H, HD)
    scores = low_back(jnp.einsum('qhd,khd->hqk', query_heads, key_heads, precision=highest) * HD ** (-0.5))
    visible = (document_row[:, None] == document_row[None, :]) & (positions[:, None] >= positions[None, :])
    scores = jnp.where(visible[None], scores, masked_score)
    shifted = jnp.exp(scores - lax.optimization_barrier(jnp.max(scores, axis=2, keepdims=True)))
    probs = shifted / lax.optimization_barrier(jnp.sum(shifted, axis=2, keepdims=True))
    attended = jnp.einsum('hqk,khd->qhd', low(probs), value_heads, precision=highest).reshape(SEQ, D)
    head_mask = ((jnp.arange(D) // HD)[None, :] < ((head_row + 1) * (H // OPTIONS))[:, None]).astype(jnp.float32)
    mixed_input = low(low_back(attended * head_mask))
    mixer_branch = low_back(jnp.dot(mixed_input, output_weight, precision=highest))
    middle = token_rows + mixer_gate[:, None] * mixer_branch
    feed_hidden = normalize(middle, feed_gain, feed_bias)
    feed_gate = route_gate(feed_hidden, feed_router, width_row)
    lifted = low_back(jnp.dot(low(feed_hidden), up_weight, precision=highest))
    width_mask = (jnp.arange(FF)[None, :] < ((width_row + 1) * (FF // OPTIONS))[:, None]).astype(jnp.float32)
    rectified = jnp.maximum(lifted, 0.0)
    activated = low(rectified * rectified * width_mask)
    feed_branch = low_back(jnp.dot(activated, down_weight, precision=highest))
    return middle + feed_gate[:, None] * feed_branch

def layer_all(token_values, weights, documents, head_level, width_level):

    def step(scan_carry, pieces):
        return (scan_carry, jax.checkpoint(sequence_layer)(weights, pieces))
    stacked = (token_values.reshape(NSEQ, SEQ, D), documents, head_level.reshape(NSEQ, SEQ), width_level.reshape(NSEQ, SEQ))
    scan_carry, layer_rows = lax.scan(step, jnp.zeros((), jnp.float32), stacked)
    return layer_rows.reshape(TOKENS, D)

def reference(tokens, documents, head_level, width_level, mixer_gain, mixer_bias, input_weight, output_weight, mixer_router, feed_gain, feed_bias, up_weight, down_weight, feed_router, cotangent):
    weights = (mixer_gain, mixer_bias, input_weight.astype(jnp.float32), output_weight.astype(jnp.float32), mixer_router, feed_gain, feed_bias, up_weight.astype(jnp.float32), down_weight.astype(jnp.float32), feed_router)

    def forward(token_values, weight_tuple):
        return layer_all(token_values, weight_tuple, documents, head_level, width_level)
    layer_out, pullback = jax.vjp(forward, tokens.astype(jnp.float32), weights)
    grad_tokens, grad_weights = pullback(cotangent.astype(jnp.float32))
    level_range = jnp.arange(OPTIONS)
    head_counts = lax.optimization_barrier(jnp.sum((head_level[:, None] == level_range[None, :]).astype(jnp.float32), axis=0))
    width_counts = lax.optimization_barrier(jnp.sum((width_level[:, None] == level_range[None, :]).astype(jnp.float32), axis=0))
    usage_counts = jnp.stack([head_counts, width_counts])
    return (layer_out.astype(jnp.bfloat16), grad_tokens, grad_weights[0], grad_weights[1], grad_weights[2], grad_weights[3], grad_weights[4], grad_weights[5], grad_weights[6], grad_weights[7], grad_weights[8], grad_weights[9], usage_counts)
```

```python
import functools

import jax
import jax.numpy as jnp
from jax import lax
from jax.experimental import pallas as pl
from jax.experimental.pallas import tpu as pltpu
from jax.sharding import Mesh, PartitionSpec as P

D = 2048
H = 16
HD = 128
FF = 8192
OPTIONS = 4
LONGEST = 512

PLANE = ("x", "y", "c")
ALL = ("z", "x", "y", "c")
GROUP = 8
SHARE = D // GROUP

highest = lax.Precision.HIGHEST
epsilon = 1e-05
masked_score = -1e30
f32 = jnp.float32
bf16 = jnp.bfloat16


def normalize(values, gain_vec, shift_vec):
    centre = values - jnp.mean(values, axis=1, keepdims=True)
    inv_scale = lax.rsqrt(jnp.mean(centre * centre, axis=1, keepdims=True) + epsilon)
    normed = centre * inv_scale
    return (normed * gain_vec + shift_vec, normed, inv_scale)


def normalize_back(grad_hidden, normed, inv_scale, gain_vec):
    grad_normed = grad_hidden * gain_vec
    inner = (
        grad_normed
        - jnp.mean(grad_normed, axis=1, keepdims=True)
        - normed * jnp.mean(grad_normed * normed, axis=1, keepdims=True)
    )
    return (inv_scale * inner, jnp.sum(grad_hidden * normed, axis=0), jnp.sum(grad_hidden, axis=0))


def route(hidden, router, picked):
    logits = jnp.dot(hidden, router, precision=highest)
    shifted = jnp.exp(logits - jnp.max(logits, axis=1, keepdims=True))
    prob_rows = shifted / jnp.sum(shifted, axis=1, keepdims=True)
    chosen = (jnp.arange(router.shape[1])[None, :] == picked[:, None]).astype(f32)
    return (router.shape[1] * jnp.sum(prob_rows * chosen, axis=1), prob_rows, chosen)


def route_back(grad_gate, prob_rows, chosen, hidden, router):
    grad_prob = router.shape[1] * grad_gate[:, None] * chosen
    grad_logits = prob_rows * (grad_prob - jnp.sum(grad_prob * prob_rows, axis=1, keepdims=True))
    grad_router = lax.dot_general(
        grad_logits, hidden, (((0,), (0,)), ((), ())), precision=highest
    )
    grad_hidden = jnp.dot(grad_logits, router.T, precision=highest)
    return (grad_router, grad_hidden)


def rope_tables(positions):
    half_width = HD // 2
    exponent = jnp.arange(half_width).astype(f32) * (-2.0 / HD)
    frequency = jnp.power(10000.0, exponent)
    angles = positions[:, None] * frequency[None, :]
    cos_half, sin_half = jnp.cos(angles), jnp.sin(angles)
    return (
        jnp.concatenate([cos_half, cos_half], axis=1),
        jnp.concatenate([-sin_half, sin_half], axis=1),
    )


def dot_plain(left, right):
    return jnp.dot(left, right, preferred_element_type=f32)


def contract_last(left, right):
    return lax.dot_general(left, right, (((1,), (1,)), ((), ())), preferred_element_type=f32)


def contract_first(left, right):
    return lax.dot_general(left, right, (((0,), (0,)), ((), ())), preferred_element_type=f32)


def flip(values, axis):
    return lax.ppermute(values, axis, [(0, 1), (1, 0)])


def plane_gather(values):
    half = values.shape[0] // 2
    from_x, from_y, from_c = flip(values, "x"), flip(values, "y"), flip(values, "c")
    diagonal = jnp.concatenate([flip(from_y[:half], "x"), flip(from_x[half:], "y")], axis=0)
    return [
        values,
        from_c,
        from_y,
        flip(from_y, "c"),
        from_x,
        flip(from_x, "c"),
        diagonal,
        flip(diagonal, "c"),
    ]


def plane_scatter(parts):
    sums = {}
    for dx in (1, 0):
        for dy in (1, 0):
            at = dx * 4 + dy * 2
            sums[dx, dy] = parts[at].astype(f32) + flip(parts[at + 1].astype(bf16), "c").astype(f32)
    half = sums[1, 1].shape[0] // 2
    diagonal = sums[1, 1].astype(bf16)
    by_x, by_y = flip(diagonal[:half], "x"), flip(diagonal[half:], "y")
    to_y = jnp.concatenate([sums[0, 1][:half] + by_x.astype(f32), sums[0, 1][half:]], axis=0)
    to_x = jnp.concatenate([sums[1, 0][:half], sums[1, 0][half:] + by_y.astype(f32)], axis=0)
    return (
        sums[0, 0]
        + flip(to_x.astype(bf16), "x").astype(f32)
        + flip(to_y.astype(bf16), "y").astype(f32)
    )


def sum_everywhere(values, planes):
    for axis in ("c", "y", "x"):
        values = values + flip(values, axis)
    if planes & (planes - 1):
        return lax.psum(values, "z")
    step = 1
    while step < planes:
        values = values + lax.ppermute(values, "z", [(i, i ^ step) for i in range(planes)])
        step *= 2
    return values


def swap_plane(values):
    return lax.all_to_all(values, PLANE, 0, 0, tiled=True)


def key_blocks(block, rows):
    return range(max(0, (block * rows - (LONGEST - 1)) // rows), block + 1)


def visible(start_col, block, key_block, rows):
    key_pos = key_block * rows + lax.broadcasted_iota(jnp.int32, (rows, rows), 1)
    seen = key_pos >= start_col
    if key_block == block:
        seen &= key_pos <= block * rows + lax.broadcasted_iota(jnp.int32, (rows, rows), 0)
    return seen


def softmax_blocks(query, rot_ref, start_col, block, rows, key_at):
    scores = []
    for key_block in key_blocks(block, rows):
        keys = rot_ref[key_block * rows : (key_block + 1) * rows, key_at : key_at + HD]
        piece = contract_last(query, keys) * HD ** (-0.5)
        scores.append(
            jnp.where(visible(start_col, block, key_block, rows), piece, masked_score)
        )
    top = functools.reduce(
        jnp.maximum, [jnp.max(piece, axis=1, keepdims=True) for piece in scores]
    )
    weights = [jnp.exp(piece - top) for piece in scores]
    total = functools.reduce(
        jnp.add, [jnp.sum(piece, axis=1, keepdims=True) for piece in weights]
    )
    inverse = 1.0 / total
    return [piece * inverse for piece in weights]


def attend_kernel(rows, blocks, place_ref, start_ref, cos_ref, sin_ref, proj_ref, rot_ref, out_ref):
    quarter = place_ref[1]
    for block in range(blocks):
        here = slice(block * rows, (block + 1) * rows)
        there = pl.ds(pl.multiple_of((block ^ quarter) * rows, rows), rows)
        cos_rows, sin_rows = cos_ref[here, :], sin_ref[here, :]
        for col in range(0, 2 * SHARE, HD):
            piece = proj_ref[there, col : col + HD]
            turned = piece * cos_rows + pltpu.roll(piece, HD // 2, 1) * sin_rows
            rot_ref[here, col : col + HD] = turned.astype(bf16)
        rot_ref[here, 2 * SHARE :] = proj_ref[there, 2 * SHARE :].astype(bf16)
    for head in range(0, SHARE, HD):
        for block in range(blocks):
            here = slice(block * rows, (block + 1) * rows)
            query = rot_ref[here, head : head + HD]
            probs = softmax_blocks(query, rot_ref, start_ref[here, :], block, rows, SHARE + head)
            total = None
            for key_block, piece in zip(key_blocks(block, rows), probs):
                values = rot_ref[
                    key_block * rows : (key_block + 1) * rows,
                    2 * SHARE + head : 2 * SHARE + head + HD,
                ]
                term = dot_plain(piece.astype(bf16), values)
                total = term if total is None else total + term
            out_ref[here, head : head + HD] = total.astype(bf16)


def attend_back_kernel(
    rows, blocks, place_ref, start_ref, cos_ref, sin_ref, rot_ref, grad_ref, out_ref, key_acc, value_acc
):
    quarter = place_ref[1]
    scale = HD ** (-0.5)

    def turn_back(piece, here):
        return piece * cos_ref[here, :] - pltpu.roll(piece, HD // 2, 1) * sin_ref[here, :]

    for head in range(0, SHARE, HD):
        key_at, value_at = SHARE + head, 2 * SHARE + head
        key_acc[...] = jnp.zeros_like(key_acc)
        value_acc[...] = jnp.zeros_like(value_acc)
        for block in range(blocks):
            here = slice(block * rows, (block + 1) * rows)
            there = pl.ds(pl.multiple_of((block ^ quarter) * rows, rows), rows)
            query = rot_ref[here, head : head + HD]
            grad = grad_ref[here, head : head + HD]
            probs = softmax_blocks(query, rot_ref, start_ref[here, :], block, rows, key_at)
            grad_probs, inner = [], None
            for key_block, piece in zip(key_blocks(block, rows), probs):
                keys_at = slice(key_block * rows, (key_block + 1) * rows)
                grad_piece = contract_last(grad, rot_ref[keys_at, value_at : value_at + HD])
                grad_probs.append(grad_piece)
                term = jnp.sum(grad_piece * piece, axis=1, keepdims=True)
                inner = term if inner is None else inner + term
            query_grad = None
            for key_block, piece, grad_piece in zip(key_blocks(block, rows), probs, grad_probs):
                keys_at = slice(key_block * rows, (key_block + 1) * rows)
                grad_scores = (piece * (grad_piece - inner)).astype(bf16)
                term = dot_plain(grad_scores, rot_ref[keys_at, key_at : key_at + HD])
                query_grad = term if query_grad is None else query_grad + term
                key_acc[keys_at, :] += contract_first(grad_scores, query)
                value_acc[keys_at, :] += contract_first(piece.astype(bf16), grad)
            out_ref[there, head : head + HD] = turn_back(query_grad * scale, here).astype(bf16)
        for block in range(blocks):
            here = slice(block * rows, (block + 1) * rows)
            there = pl.ds(pl.multiple_of((block ^ quarter) * rows, rows), rows)
            out_ref[there, key_at : key_at + HD] = turn_back(
                key_acc[here, :] * scale, here
            ).astype(bf16)
            out_ref[there, value_at : value_at + HD] = value_acc[here, :].astype(bf16)


def attend(place, starts, cos_table, sin_table, projected, rows):
    seq_rows = cos_table.shape[0]
    body = functools.partial(attend_kernel, rows, seq_rows // rows)
    return pl.pallas_call(
        body,
        grid_spec=pltpu.PrefetchScalarGridSpec(
            num_scalar_prefetch=1,
            grid=(2,),
            in_specs=[
                pl.BlockSpec((None, seq_rows, 1), lambda s, place: (s ^ place[0], 0, 0)),
                pl.BlockSpec((seq_rows, HD), lambda s, place: (0, 0)),
                pl.BlockSpec((seq_rows, HD), lambda s, place: (0, 0)),
                pl.BlockSpec((seq_rows, 3 * SHARE), lambda s, place: (s, 0)),
            ],
            out_specs=[
                pl.BlockSpec((seq_rows, 3 * SHARE), lambda s, place: (s, 0)),
                pl.BlockSpec((seq_rows, SHARE), lambda s, place: (s ^ place[0], 0)),
            ],
        ),
        out_shape=[
            jax.ShapeDtypeStruct((2 * seq_rows, 3 * SHARE), bf16),
            jax.ShapeDtypeStruct((2 * seq_rows, SHARE), bf16),
        ],
        compiler_params=pltpu.CompilerParams(vmem_limit_bytes=48 * 1024 * 1024),
        cost_estimate=pl.CostEstimate(
            flops=4 * 4 * seq_rows * seq_rows * HD, bytes_accessed=16 * 2**20, transcendentals=2**21
        ),
    )(place, starts, cos_table, sin_table, projected)


def attend_back(place, starts, cos_table, sin_table, rotated, grad, rows):
    seq_rows = cos_table.shape[0]
    body = functools.partial(attend_back_kernel, rows, seq_rows // rows)
    return pl.pallas_call(
        body,
        grid_spec=pltpu.PrefetchScalarGridSpec(
            num_scalar_prefetch=1,
            grid=(2,),
            in_specs=[
                pl.BlockSpec((None, seq_rows, 1), lambda s, place: (s ^ place[0], 0, 0)),
                pl.BlockSpec((seq_rows, HD), lambda s, place: (0, 0)),
                pl.BlockSpec((seq_rows, HD), lambda s, place: (0, 0)),
                pl.BlockSpec((seq_rows, 3 * SHARE), lambda s, place: (s, 0)),
                pl.BlockSpec((seq_rows, SHARE), lambda s, place: (s ^ place[0], 0)),
            ],
            out_specs=pl.BlockSpec((seq_rows, 3 * SHARE), lambda s, place: (s, 0)),
            scratch_shapes=[pltpu.VMEM((seq_rows, HD), f32), pltpu.VMEM((seq_rows, HD), f32)],
        ),
        out_shape=jax.ShapeDtypeStruct((2 * seq_rows, 3 * SHARE), bf16),
        compiler_params=pltpu.CompilerParams(vmem_limit_bytes=48 * 1024 * 1024),
        cost_estimate=pl.CostEstimate(
            flops=10 * 4 * seq_rows * seq_rows * HD, bytes_accessed=16 * 2**20, transcendentals=2**21
        ),
    )(place, starts, cos_table, sin_table, rotated, grad)


def local(
    planes,
    tokens,
    documents,
    head_level,
    width_level,
    mixer_gain,
    mixer_bias,
    input_weight,
    output_weight,
    mixer_router,
    feed_gain,
    feed_bias,
    up_weight,
    down_weight,
    feed_router,
    cotangent,
):
    rows = tokens.shape[0]
    seq_rows = documents.shape[1]
    quarters = seq_rows // rows
    weight_rows = input_weight.shape[0]
    unit_rows = down_weight.shape[0]
    at_x = lax.axis_index("x")
    quarter = lax.axis_index("y") * 2 + lax.axis_index("c")
    at_plane = at_x * quarters + quarter
    place = jnp.stack([at_x, quarter]).astype(jnp.int32)
    chunk_order = at_plane ^ jnp.arange(GROUP)

    whole = lax.all_gather(
        jnp.concatenate([documents[0], width_level])[None], PLANE, axis=0, tiled=True
    )
    plane_docs = jnp.stack([whole[0, :seq_rows], whole[quarters, :seq_rows]])
    width_all = whole[:, seq_rows:][chunk_order].reshape(GROUP * rows)
    starts = jnp.sum(
        (plane_docs[:, None, :] < plane_docs[:, :, None]).astype(jnp.int32), axis=2
    )[:, :, None]
    level_range = jnp.arange(OPTIONS)
    head_counts = jnp.sum((head_level[:, None] == level_range[None, :]).astype(f32), axis=0)
    width_counts = jnp.sum((width_level[:, None] == level_range[None, :]).astype(f32), axis=0)

    input_share = swap_plane(
        input_weight.reshape(weight_rows, 3, GROUP, SHARE)
        .transpose(2, 0, 1, 3)
        .reshape(GROUP * weight_rows, 3 * SHARE)
    )
    input_share = lax.all_gather(input_share, "z", axis=0, tiled=True)
    output_full = lax.all_gather(output_weight, ALL, axis=0, tiled=True)
    up_share = swap_plane(
        up_weight.reshape(weight_rows, planes, GROUP, unit_rows)
        .transpose(2, 0, 1, 3)
        .reshape(GROUP * weight_rows, planes * unit_rows)
    )
    up_share = lax.all_gather(up_share, "z", axis=0, tiled=True)
    down_share = lax.all_gather(down_weight, "z", axis=0, tiled=True)

    token_values = tokens.astype(f32)
    mixer_hidden, mixer_normed, mixer_scale = normalize(token_values, mixer_gain, mixer_bias)
    mixer_gate, mixer_probs, mixer_chosen = route(mixer_hidden, mixer_router, head_level)
    mixer_all = jnp.concatenate(plane_gather(mixer_hidden.astype(bf16)), axis=0)
    projected = dot_plain(mixer_all, input_share)
    cos_table, sin_table = rope_tables(jnp.arange(seq_rows).astype(f32))
    rotated, attended = attend(place, starts, cos_table, sin_table, projected, rows)

    def by_token(values):
        return (
            swap_plane(values).reshape(GROUP, rows, SHARE).transpose(1, 0, 2).reshape(rows, D)
        )

    def by_head(values):
        return swap_plane(
            values.reshape(rows, GROUP, SHARE).transpose(1, 0, 2).reshape(GROUP * rows, SHARE)
        )

    head_mask = (
        (jnp.arange(D) // HD)[None, :] < ((head_level + 1) * (H // OPTIONS))[:, None]
    ).astype(bf16)
    mixed_input = by_token(attended) * head_mask
    mixer_branch = dot_plain(mixed_input, output_full)
    middle = token_values + mixer_gate[:, None] * mixer_branch
    feed_hidden, feed_normed, feed_scale = normalize(middle, feed_gain, feed_bias)
    feed_gate, feed_probs, feed_chosen = route(feed_hidden, feed_router, width_level)
    upstream = cotangent.astype(f32)

    feed_all = jnp.concatenate(plane_gather(feed_hidden.astype(bf16)), axis=0)
    upstream_all = jnp.concatenate(plane_gather(cotangent), axis=0)
    gate_all = jnp.concatenate(plane_gather(feed_gate.reshape(2, rows // 2)), axis=0).reshape(
        GROUP * rows
    )
    lifted = dot_plain(feed_all, up_share)
    unit = jnp.arange(planes * unit_rows)
    unit = (unit // unit_rows * GROUP + at_plane) * unit_rows + unit % unit_rows
    width_mask = (unit[None, :] < ((width_all + 1) * (FF // OPTIONS))[:, None]).astype(f32)
    rectified = jnp.maximum(lifted, 0.0)
    activated = (rectified * rectified * width_mask).astype(bf16)

    def pieces(values):
        return [values[d * rows : (d + 1) * rows] for d in range(GROUP)]

    feed_branch = plane_scatter(pieces(dot_plain(activated, down_share).astype(bf16)))
    grad_branch_all = (gate_all[:, None] * upstream_all.astype(f32)).astype(bf16)
    grad_activated = contract_last(grad_branch_all, down_share)
    grad_lifted = (grad_activated * width_mask * 2.0 * rectified).astype(bf16)
    grad_feed_input = plane_scatter(pieces(contract_last(grad_lifted, up_share).astype(bf16)))
    grad_down_weight = lax.psum_scatter(
        contract_first(activated, grad_branch_all).astype(bf16),
        "z",
        scatter_dimension=0,
        tiled=True,
    ).astype(f32)
    up_part = swap_plane(
        lax.psum_scatter(
            contract_first(feed_all, grad_lifted).astype(bf16),
            "z",
            scatter_dimension=0,
            tiled=True,
        )
    )
    grad_up_weight = (
        up_part.reshape(GROUP, weight_rows, planes, unit_rows)
        .transpose(1, 2, 0, 3)
        .reshape(weight_rows, FF)
        .astype(f32)
    )

    outputs = (middle + feed_gate[:, None] * feed_branch).astype(bf16)
    grad_feed_gate = jnp.sum(feed_branch * upstream, axis=1)
    feed_router_term, grad_feed_routed = route_back(
        grad_feed_gate, feed_probs, feed_chosen, feed_hidden, feed_router
    )
    grad_middle_norm, feed_gain_term, feed_bias_term = normalize_back(
        grad_feed_input + grad_feed_routed, feed_normed, feed_scale, feed_gain
    )
    grad_middle = upstream + grad_middle_norm
    grad_mixer_gate = jnp.sum(mixer_branch * grad_middle, axis=1)
    grad_mixer_branch = (mixer_gate[:, None] * grad_middle).astype(bf16)
    grad_attended = contract_last(grad_mixer_branch, output_full).astype(bf16) * head_mask
    grad_output_weight = lax.psum_scatter(
        contract_first(mixed_input, grad_mixer_branch).astype(bf16),
        ALL,
        scatter_dimension=0,
        tiled=True,
    ).astype(f32)
    grad_projected = attend_back(
        place, starts, cos_table, sin_table, rotated, by_head(grad_attended), rows
    )
    grad_mixer_input = plane_scatter(
        pieces(contract_last(grad_projected, input_share).astype(bf16))
    )
    input_part = swap_plane(
        lax.psum_scatter(
            contract_first(mixer_all, grad_projected).astype(bf16),
            "z",
            scatter_dimension=0,
            tiled=True,
        )
    )
    grad_input_weight = (
        input_part.reshape(GROUP, weight_rows, 3, SHARE)
        .transpose(1, 2, 0, 3)
        .reshape(weight_rows, 3 * D)
        .astype(f32)
    )
    mixer_router_term, grad_mixer_routed = route_back(
        grad_mixer_gate, mixer_probs, mixer_chosen, mixer_hidden, mixer_router
    )
    grad_token_norm, mixer_gain_term, mixer_bias_term = normalize_back(
        grad_mixer_input + grad_mixer_routed, mixer_normed, mixer_scale, mixer_gain
    )
    grad_tokens = grad_middle + grad_token_norm

    counts = jnp.pad(jnp.concatenate([head_counts, width_counts]), (0, D - 2 * OPTIONS))
    feed_sums = sum_everywhere(
        jnp.concatenate(
            [feed_gain_term[None], feed_bias_term[None], feed_router_term, counts[None]], axis=0
        ),
        planes,
    )
    mixer_sums = sum_everywhere(
        jnp.concatenate(
            [mixer_gain_term[None], mixer_bias_term[None], mixer_router_term], axis=0
        ),
        planes,
    )
    return (
        outputs,
        grad_tokens,
        mixer_sums[0],
        mixer_sums[1],
        grad_input_weight,
        grad_output_weight,
        mixer_sums[2:6].T,
        feed_sums[0],
        feed_sums[1],
        grad_up_weight,
        grad_down_weight,
        feed_sums[2:6].T,
        feed_sums[6, : 2 * OPTIONS].reshape(2, OPTIONS),
    )


def solution(mesh):
    wide, narrow = mesh.shape["wide"], mesh.shape["narrow"]
    planes = wide // 2
    inner = Mesh(mesh.devices.reshape(planes, 2, narrow // 2, 2), ALL)
    rowwise = P(ALL, None)
    in_specs = (
        rowwise,
        P(("z", "x"), None),
        P(ALL),
        P(ALL),
        P(),
        P(),
        rowwise,
        rowwise,
        P(),
        P(),
        P(),
        rowwise,
        rowwise,
        P(),
        rowwise,
    )
    out_specs = (
        rowwise,
        rowwise,
        P(),
        P(),
        rowwise,
        rowwise,
        P(),
        P(),
        P(),
        rowwise,
        rowwise,
        P(),
        P(),
    )
    return jax.shard_map(
        functools.partial(local, planes),
        mesh=inner,
        in_specs=in_specs,
        out_specs=out_specs,
        check_vma=False,
    )
```

```python
import functools

import jax
import jax.numpy as jnp
from jax import lax
from jax.experimental import pallas as pl
from jax.experimental.pallas import tpu as pltpu
from jax.sharding import Mesh, PartitionSpec as P

D = 2048
H = 16
HD = 128
FF = 8192
OPTIONS = 4
LONGEST = 512

PLANE = ("x", "y", "c")
ALL = ("z", "x", "y", "c")
GROUP = 8
SHARE = D // GROUP

highest = lax.Precision.HIGHEST
epsilon = 1e-05
masked_score = -1e30
f32 = jnp.float32
bf16 = jnp.bfloat16


def normalize(values, gain_vec, shift_vec):
    centre = values - jnp.mean(values, axis=1, keepdims=True)
    inv_scale = lax.rsqrt(jnp.mean(centre * centre, axis=1, keepdims=True) + epsilon)
    normed = centre * inv_scale
    return (normed * gain_vec + shift_vec, normed, inv_scale)


def normalize_back(grad_hidden, normed, inv_scale, gain_vec):
    grad_normed = grad_hidden * gain_vec
    inner = (
        grad_normed
        - jnp.mean(grad_normed, axis=1, keepdims=True)
        - normed * jnp.mean(grad_normed * normed, axis=1, keepdims=True)
    )
    return (inv_scale * inner, jnp.sum(grad_hidden * normed, axis=0), jnp.sum(grad_hidden, axis=0))


def route(hidden, router, picked):
    logits = jnp.dot(hidden, router, precision=highest)
    shifted = jnp.exp(logits - jnp.max(logits, axis=1, keepdims=True))
    prob_rows = shifted / jnp.sum(shifted, axis=1, keepdims=True)
    chosen = (jnp.arange(router.shape[1])[None, :] == picked[:, None]).astype(f32)
    return (router.shape[1] * jnp.sum(prob_rows * chosen, axis=1), prob_rows, chosen)


def route_back(grad_gate, prob_rows, chosen, hidden, router):
    grad_prob = router.shape[1] * grad_gate[:, None] * chosen
    grad_logits = prob_rows * (grad_prob - jnp.sum(grad_prob * prob_rows, axis=1, keepdims=True))
    grad_router = lax.dot_general(
        grad_logits, hidden, (((0,), (0,)), ((), ())), precision=highest
    )
    grad_hidden = jnp.dot(grad_logits, router.T, precision=highest)
    return (grad_router, grad_hidden)


def rope_tables(positions):
    half_width = HD // 2
    exponent = jnp.arange(half_width).astype(f32) * (-2.0 / HD)
    frequency = jnp.power(10000.0, exponent)
    angles = positions[:, None] * frequency[None, :]
    cos_half, sin_half = jnp.cos(angles), jnp.sin(angles)
    return (
        jnp.concatenate([cos_half, cos_half], axis=1),
        jnp.concatenate([-sin_half, sin_half], axis=1),
    )


def dot_plain(left, right):
    return jnp.dot(left, right, preferred_element_type=f32)


def contract_last(left, right):
    return lax.dot_general(left, right, (((1,), (1,)), ((), ())), preferred_element_type=f32)


def contract_first(left, right):
    return lax.dot_general(left, right, (((0,), (0,)), ((), ())), preferred_element_type=f32)


def flip(values, axis):
    return lax.ppermute(values, axis, [(0, 1), (1, 0)])


def gather_four(values):
    half = values.shape[0] // 2
    top, bottom = values[:half], values[half:]
    y_top, x_bottom = flip(top, "y"), flip(bottom, "x")
    y_bottom, x_top = flip(bottom, "y"), flip(top, "x")
    return [values, y_top, y_bottom, x_top, x_bottom, flip(y_top, "x"), flip(x_bottom, "y")]


def gather_eight(values):
    chunks = gather_four(values)
    return chunks + [flip(chunk, "c") for chunk in chunks]


def copies_in(pieces, whole, sem):
    copies, at = [], 0
    for i, piece in enumerate(pieces):
        count = piece.shape[0]
        copies.append(pltpu.make_async_copy(piece, whole.at[at : at + count, :], sem.at[i]))
        at += count
    return copies


def scatter_send(parts):
    half = parts[0].shape[0] // 2
    by_x, by_y = flip(parts[3][:half], "x"), flip(parts[3][half:], "y")
    x_top, y_bottom = flip(parts[2][:half], "x"), flip(parts[1][half:], "y")
    return by_x, by_y, x_top, y_bottom


def scatter_end(parts, sent):
    half = parts[0].shape[0] // 2
    by_x, by_y, x_top, y_bottom = sent
    y_top = flip((parts[1][:half].astype(f32) + by_x.astype(f32)).astype(bf16), "y")
    x_bottom = flip((parts[2][half:].astype(f32) + by_y.astype(f32)).astype(bf16), "x")
    own = parts[0].astype(f32)
    return jnp.concatenate(
        [
            own[:half] + x_top.astype(f32) + y_top.astype(f32),
            own[half:] + x_bottom.astype(f32) + y_bottom.astype(f32),
        ],
        axis=0,
    )


def scatter_four(parts):
    return scatter_end(parts, scatter_send(parts))


def add_cores(parts):
    other = [flip(part, "c") for part in parts[4:]]
    return [(a.astype(f32) + b.astype(f32)).astype(bf16) for a, b in zip(parts[:4], other)]


def send_four(values, d):
    return lax.ppermute(values, ("x", "y"), [(i, i ^ d) for i in range(4)])


def gather_small(values):
    return jnp.stack([values] + [send_four(values, d) for d in range(1, 4)])


def sum_small(values):
    return values[0] + sum(send_four(values[d], d) for d in range(1, 4))


def sum_everywhere(values, planes, before_last):
    for axis in ("c", "y", "x"):
        values = values + flip(values, axis)
    if planes & (planes - 1):
        return lax.psum(values, "z"), before_last
    step = 1
    while step < planes:
        if 2 * step == planes:
            values, before_last = lax.optimization_barrier((values, before_last))
        values = values + lax.ppermute(values, "z", [(i, i ^ step) for i in range(planes)])
        step *= 2
    return values, before_last


def after(values, *others):
    return lax.optimization_barrier((values, *others))[0]


def head_numbers():
    chip = lax.axis_index("x") * 2 + lax.axis_index("y")
    return [chip + 4 * (2 * lax.axis_index("c") + e) for e in range(2)]


def by_core(mine, other, axis):
    return jnp.where(
        lax.axis_index("c") == 0,
        jnp.concatenate([mine, other], axis=axis),
        jnp.concatenate([other, mine], axis=axis),
    )


def share_heads(blocks):
    weight_rows = blocks[0].shape[0]
    if len(blocks) == 1 or 2 * weight_rows != HD:
        full = lax.all_gather(blocks[0], ALL, axis=0, tiled=True)
        mine = [lax.dynamic_slice_in_dim(full, h * HD, HD, 0) for h in head_numbers()]
        mine = jnp.concatenate(mine, axis=0)
        return jnp.concatenate([mine, flip(mine, "c")], axis=0)
    halves = jnp.zeros((len(blocks), 1, weight_rows, D), bf16)
    for d, block in enumerate(blocks):
        at = lax.axis_index("z") ^ d
        halves = lax.dynamic_update_slice(halves, block[None, None], (at, 0, 0, 0))
    heads = by_core(halves, flip(halves, "c"), 1)
    core = lax.axis_index("c")
    return jnp.concatenate(
        [
            lax.dynamic_slice_in_dim(heads, 2 * core, 2, 0),
            lax.dynamic_slice_in_dim(heads, 2 - 2 * core, 2, 0),
        ],
        axis=0,
    ).reshape(2 * SHARE, D)


def sum_heads(part, planes, weight_rows):
    if 2 * weight_rows != HD:
        mine = part[:SHARE] + flip(part[SHARE:], "c")
        full = jnp.zeros((D, D), part.dtype)
        for e, h in enumerate(head_numbers()):
            full = lax.dynamic_update_slice(full, mine[e * HD : (e + 1) * HD], (h * HD, 0))
        return lax.psum_scatter(full, ALL, scatter_dimension=0, tiled=True)
    core = lax.axis_index("c")
    halves = part.reshape(4, 2, weight_rows, D)
    mine = lax.dynamic_slice_in_dim(halves, core, 1, 1)[:, 0]
    other = flip(lax.dynamic_slice_in_dim(halves, 1 - core, 1, 1)[:, 0], "c")
    first = (mine[:2].astype(f32) + other[2:].astype(f32)).astype(bf16)
    second = (mine[2:].astype(f32) + other[:2].astype(f32)).astype(bf16)
    return lax.psum_scatter(
        by_core(first, second, 0).reshape(planes * weight_rows, D),
        "z",
        scatter_dimension=0,
        tiled=True,
    )


def attention_columns():
    return [
        (part * D + (p // 2 + 4 * (2 * (p % 2) + e)) * HD, HD, p, (e * 3 + part) * HD)
        for p in range(GROUP)
        for part in range(3)
        for e in range(2)
    ]


def unit_columns(planes, unit_rows):
    return [
        ((k * GROUP + p) * unit_rows, unit_rows, p, k * unit_rows)
        for p in range(GROUP)
        for k in range(planes)
    ]


def deal_kernel(moves, whole_ref, dealt_ref):
    for first, width, p, at in moves:
        dealt_ref[p, :, at : at + width] = whole_ref[:, first : first + width]


def deal(whole, moves):
    rows, columns = whole.shape
    if any(width % 128 for _, width, _, _ in moves):
        parts = [[] for _ in range(GROUP)]
        for first, width, p, _ in moves:
            parts[p].append(whole[:, first : first + width])
        return jnp.concatenate([jnp.concatenate(part, axis=1) for part in parts], axis=0)
    dealt = pl.pallas_call(
        functools.partial(deal_kernel, moves),
        out_shape=jax.ShapeDtypeStruct((GROUP, rows, columns // GROUP), whole.dtype),
    )(whole)
    return dealt.reshape(GROUP * rows, columns // GROUP)


def undeal_kernel(moves, dealt_ref, whole_ref):
    for first, width, p, at in moves:
        whole_ref[:, first : first + width] = dealt_ref[p, :, at : at + width].astype(f32)


def undeal(dealt, moves):
    rows, columns = dealt.shape[0] // GROUP, dealt.shape[1] * GROUP
    dealt = dealt.reshape(GROUP, rows, columns // GROUP)
    if any(width % 128 for _, width, _, _ in moves):
        return jnp.concatenate(
            [dealt[p, :, at : at + width] for _, width, p, at in sorted(moves)], axis=1
        ).astype(f32)
    return pl.pallas_call(
        functools.partial(undeal_kernel, moves),
        out_shape=jax.ShapeDtypeStruct((rows, columns), f32),
    )(dealt)


def swap_plane(values):
    return lax.all_to_all(values, PLANE, 0, 0, tiled=True)


def chunk_at(block, quarter, rows):
    differs = block ^ quarter
    return differs % 2, pl.ds(pl.multiple_of(differs // 2 * rows, rows), rows)


def key_blocks(block, rows):
    return range(max(0, (block * rows - (LONGEST - 1)) // rows), block + 1)


def visible(start_col, block, key_block, rows):
    key_pos = key_block * rows + lax.broadcasted_iota(jnp.int32, (rows, rows), 1)
    seen = key_pos >= start_col
    if key_block == block:
        seen &= key_pos <= block * rows + lax.broadcasted_iota(jnp.int32, (rows, rows), 0)
    return seen


def softmax_blocks(query, rot_ref, start_col, block, rows, key_at):
    scores = []
    for key_block in key_blocks(block, rows):
        keys = rot_ref[key_block * rows : (key_block + 1) * rows, key_at : key_at + HD]
        piece = contract_last(query, keys) * HD ** (-0.5)
        scores.append(
            jnp.where(visible(start_col, block, key_block, rows), piece, masked_score)
        )
    top = functools.reduce(
        jnp.maximum, [jnp.max(piece, axis=1, keepdims=True) for piece in scores]
    )
    weights = [jnp.exp(piece - top) for piece in scores]
    total = functools.reduce(
        jnp.add, [jnp.sum(piece, axis=1, keepdims=True) for piece in weights]
    )
    inverse = 1.0 / total
    return [piece * inverse for piece in weights]


def attend_kernel(
    rows,
    blocks,
    head,
    place_ref,
    start_ref,
    level_ref,
    cos_ref,
    sin_ref,
    weight_ref,
    *others,
):
    pieces, others = others[:-6], others[-6:]
    rot_ref, out_ref, all_ref, hidden_ref, sem, out_sem = others
    quarter = place_ref[0]
    level_least = place_ref[1]
    sequence = pl.program_id(0)
    copies = copies_in(pieces, hidden_ref, sem)
    copy_out = pltpu.make_async_copy(hidden_ref, all_ref, out_sem)
    first = [copies[i] for i in (0, 1, 2, 7, 8, 9)]
    second = [copies[i] for i in (3, 4, 5, 6, 10, 11, 12, 13)]

    @pl.when(sequence == 0)
    def _():
        for copy in first + second:
            copy.start()
        for copy in first:
            copy.wait()

    @pl.when(sequence == 1)
    def _():
        for copy in second:
            copy.wait()
        copy_out.start()

    for block in range(blocks):
        here = slice(block * rows, (block + 1) * rows)
        other, there = chunk_at(block, quarter, rows)
        cos_rows, sin_rows = cos_ref[here, :], sin_ref[here, :]
        at = (other * 4 + sequence * 2 + (block ^ quarter) // 2) * rows
        hidden = hidden_ref[pl.ds(pl.multiple_of(at, rows), rows), :]
        projected = dot_plain(hidden, weight_ref[...])
        for col in range(0, 2 * HD, HD):
            piece = projected[:, col : col + HD]
            turned = piece * cos_rows + pltpu.roll(piece, HD // 2, 1) * sin_rows
            rot_ref[here, col : col + HD] = turned.astype(bf16)
        rot_ref[here, 2 * HD :] = projected[:, 2 * HD :].astype(bf16)
    for block in range(blocks):
        here = slice(block * rows, (block + 1) * rows)
        other, there = chunk_at(block, quarter, rows)
        query = rot_ref[here, :HD]
        probs = softmax_blocks(query, rot_ref, start_ref[here, :], block, rows, HD)
        total = None
        for key_block, piece in zip(key_blocks(block, rows), probs):
            values = rot_ref[key_block * rows : (key_block + 1) * rows, 2 * HD :]
            term = dot_plain(piece.astype(bf16), values)
            total = term if total is None else total + term
        kept = level_ref[other, there, :] >= level_least + head
        out_ref[other, there, :] = jnp.where(kept, total, 0.0).astype(bf16)

    @pl.when(sequence == 1)
    def _():
        copy_out.wait()


def attend_back_kernel(
    rows,
    blocks,
    place_ref,
    start_ref,
    level_ref,
    cos_ref,
    sin_ref,
    rot_refs_0,
    rot_refs_1,
    grad_ref,
    weight_0,
    weight_1,
    out_ref,
    hidden_ref,
    key_acc,
    value_acc,
):
    quarter = place_ref[0]
    level_least = place_ref[1]
    scale = HD ** (-0.5)

    def turn_back(piece, here):
        return piece * cos_ref[here, :] - pltpu.roll(piece, HD // 2, 1) * sin_ref[here, :]

    for head, rot_ref in ((0, rot_refs_0), (HD, rot_refs_1)):
        key_at, value_at = HD, 2 * HD
        out_at = head * 3
        key_acc[...] = jnp.zeros_like(key_acc)
        value_acc[...] = jnp.zeros_like(value_acc)
        for block in range(blocks):
            here = slice(block * rows, (block + 1) * rows)
            other, there = chunk_at(block, quarter, rows)
            query = rot_ref[here, :HD]
            kept = level_ref[other, there, :] >= level_least + head // HD
            grad = jnp.where(kept, grad_ref[other, there, head : head + HD], 0.0).astype(bf16)
            probs = softmax_blocks(query, rot_ref, start_ref[here, :], block, rows, key_at)
            grad_probs, inner = [], None
            for key_block, piece in zip(key_blocks(block, rows), probs):
                keys_at = slice(key_block * rows, (key_block + 1) * rows)
                grad_piece = contract_last(grad, rot_ref[keys_at, value_at : value_at + HD])
                grad_probs.append(grad_piece)
                term = jnp.sum(grad_piece * piece, axis=1, keepdims=True)
                inner = term if inner is None else inner + term
            query_grad = None
            for key_block, piece, grad_piece in zip(key_blocks(block, rows), probs, grad_probs):
                keys_at = slice(key_block * rows, (key_block + 1) * rows)
                grad_scores = (piece * (grad_piece - inner)).astype(bf16)
                term = dot_plain(grad_scores, rot_ref[keys_at, key_at : key_at + HD])
                query_grad = term if query_grad is None else query_grad + term
                key_acc[keys_at, :] += contract_first(grad_scores, query)
                value_acc[keys_at, :] += contract_first(piece.astype(bf16), grad)
            out_ref[other, there, out_at : out_at + HD] = turn_back(query_grad * scale, here).astype(bf16)
        for block in range(blocks):
            here = slice(block * rows, (block + 1) * rows)
            other, there = chunk_at(block, quarter, rows)
            out_ref[other, there, out_at + HD : out_at + 2 * HD] = turn_back(
                key_acc[here, :] * scale, here
            ).astype(bf16)
            out_ref[other, there, out_at + 2 * HD : out_at + 3 * HD] = value_acc[
                here, :
            ].astype(bf16)
    for block in range(blocks):
        other, there = chunk_at(block, quarter, rows)
        hidden_ref[other, there, :] = (
            contract_last(out_ref[other, there, : 3 * HD], weight_0[...])
            + contract_last(out_ref[other, there, 3 * HD :], weight_1[...])
        ).astype(bf16)


def chunked(seq_rows, columns):
    return pl.BlockSpec((2, None, seq_rows // 2, columns), lambda s, place: (0, s, 0, 0))


def attend(place, starts, levels, cos_table, sin_table, weight, pieces, rows, head):
    seq_rows = cos_table.shape[0]
    body = functools.partial(attend_kernel, rows, seq_rows // rows, head)
    return pl.pallas_call(
        body,
        grid_spec=pltpu.PrefetchScalarGridSpec(
            num_scalar_prefetch=1,
            grid=(2,),
            in_specs=[
                pl.BlockSpec((seq_rows, 1), lambda s, place: (s, 0)),
                chunked(seq_rows, 1),
                pl.BlockSpec((seq_rows, HD), lambda s, place: (0, 0)),
                pl.BlockSpec((seq_rows, HD), lambda s, place: (0, 0)),
                pl.BlockSpec((D, 3 * HD), lambda s, place: (0, 0)),
            ]
            + [pl.BlockSpec(memory_space=pl.ANY)] * len(pieces),
            out_specs=[
                pl.BlockSpec((seq_rows, 3 * HD), lambda s, place: (s, 0)),
                chunked(seq_rows, HD),
                pl.BlockSpec(memory_space=pl.ANY),
            ],
            scratch_shapes=[
                pltpu.VMEM((2 * seq_rows, D), bf16),
                pltpu.SemaphoreType.DMA((len(pieces),)),
                pltpu.SemaphoreType.DMA,
            ],
        ),
        out_shape=[
            jax.ShapeDtypeStruct((2 * seq_rows, 3 * HD), bf16),
            jax.ShapeDtypeStruct((2, 2, seq_rows // 2, HD), bf16),
            jax.ShapeDtypeStruct((2 * seq_rows, D), bf16),
        ],
        compiler_params=pltpu.CompilerParams(vmem_limit_bytes=48 * 1024 * 1024),
    )(
        place,
        starts,
        levels,
        cos_table,
        sin_table,
        weight,
        *pieces,
    )


def attend_back(place, starts, levels, cos_table, sin_table, rotated, grad, weights, rows):
    seq_rows = cos_table.shape[0]
    body = functools.partial(attend_back_kernel, rows, seq_rows // rows)
    grad_projected, grad_hidden = pl.pallas_call(
        body,
        grid_spec=pltpu.PrefetchScalarGridSpec(
            num_scalar_prefetch=1,
            grid=(2,),
            in_specs=[
                pl.BlockSpec((seq_rows, 1), lambda s, place: (s, 0)),
                chunked(seq_rows, 1),
                pl.BlockSpec((seq_rows, HD), lambda s, place: (0, 0)),
                pl.BlockSpec((seq_rows, HD), lambda s, place: (0, 0)),
                pl.BlockSpec((seq_rows, 3 * HD), lambda s, place: (s, 0)),
                pl.BlockSpec((seq_rows, 3 * HD), lambda s, place: (s, 0)),
                chunked(seq_rows, SHARE),
                pl.BlockSpec((D, 3 * HD), lambda s, place: (0, 0)),
                pl.BlockSpec((D, 3 * HD), lambda s, place: (0, 0)),
            ],
            out_specs=[chunked(seq_rows, 3 * SHARE), chunked(seq_rows, D)],
            scratch_shapes=[pltpu.VMEM((seq_rows, HD), f32), pltpu.VMEM((seq_rows, HD), f32)],
        ),
        out_shape=[
            jax.ShapeDtypeStruct((2, 2, seq_rows // 2, 3 * SHARE), bf16),
            jax.ShapeDtypeStruct((2, 2, seq_rows // 2, D), bf16),
        ],
        compiler_params=pltpu.CompilerParams(vmem_limit_bytes=48 * 1024 * 1024),
    )(
        place,
        starts,
        levels,
        cos_table,
        sin_table,
        *rotated,
        grad.reshape(2, 2, seq_rows // 2, SHARE),
        *weights,
    )
    return (
        grad_projected.reshape(2 * seq_rows, 3 * SHARE),
        grad_hidden.reshape(2 * seq_rows, D),
    )


BLOCK = 512
NARROW = 512


def narrower(block):
    wide = min(NARROW, block)
    return [slice(at, at + wide) for at in range(0, block, wide)]


def of_two(step, half, body, mine_ref, other_ref):
    @pl.when(step < half)
    def _():
        body(mine_ref)

    @pl.when(step >= half)
    def _():
        body(other_ref)


def lift_kernel(half, gate_ref, limit_ref, unit_ref, mine_ref, other_ref, *others):
    feed_pieces, upstream_pieces = others[:7], others[7:14]
    rectified_ref, activated_ref, grad_ref, feed_all, upstream_all = others[14:19]
    feed_ref, upstream_ref, feed_sem, upstream_sem, out_sem = others[19:]
    step = pl.program_id(0)
    wide = grad_ref.shape[1]
    feed_in = copies_in(feed_pieces, feed_ref, feed_sem)
    upstream_in = copies_in(upstream_pieces, upstream_ref, upstream_sem)
    feed_out = pltpu.make_async_copy(feed_ref, feed_all, out_sem.at[0])
    upstream_out = pltpu.make_async_copy(upstream_ref, upstream_all, out_sem.at[1])

    @pl.when(step == 0)
    def _():
        for copy in feed_in + upstream_in:
            copy.start()
        for copy in feed_in:
            copy.wait()
        feed_out.start()

    def body(up_ref):
        for at in narrower(rectified_ref.shape[1]):
            kept = unit_ref[:, at] < limit_ref[...]
            lifted = dot_plain(feed_ref[...], up_ref[:, at])
            rectified = jnp.where(kept, jnp.maximum(lifted, 0.0), 0.0)
            rectified_ref[:, at] = rectified
            activated_ref[:, at] = (rectified * rectified).astype(bf16)

    of_two(step, half, body, mine_ref, other_ref)

    @pl.when(step == 0)
    def _():
        for copy in upstream_in:
            copy.wait()
        upstream_out.start()

    upstream = upstream_ref[:, pl.ds(pl.multiple_of(step * wide, wide), wide)]
    grad_ref[...] = (gate_ref[...] * upstream.astype(f32)).astype(bf16)

    @pl.when(step == 2 * half - 1)
    def _():
        feed_out.wait()
        upstream_out.wait()


def lift(gate, limit, unit, up_mine, up_other, feed, upstream):
    count, units = gate.shape[0], up_mine.shape[1]
    block = min(BLOCK, units)
    half = units // block
    steps = 2 * half
    wide = D // steps
    return pl.pallas_call(
        functools.partial(lift_kernel, half),
        grid=(steps,),
        in_specs=[
            pl.BlockSpec((count, 1), lambda s: (0, 0)),
            pl.BlockSpec((count, 1), lambda s: (0, 0)),
            pl.BlockSpec((1, block), lambda s: (0, s)),
            pl.BlockSpec((D, block), lambda s: (0, jnp.minimum(s, half - 1))),
            pl.BlockSpec((D, block), lambda s: (0, jnp.maximum(s - half, 0))),
        ]
        + [pl.BlockSpec(memory_space=pl.ANY)] * 14,
        out_specs=[
            pl.BlockSpec((count, block), lambda s: (0, s)),
            pl.BlockSpec((count, block), lambda s: (0, s)),
            pl.BlockSpec((count, wide), lambda s: (0, s)),
            pl.BlockSpec(memory_space=pl.ANY),
            pl.BlockSpec(memory_space=pl.ANY),
        ],
        out_shape=[
            jax.ShapeDtypeStruct((count, 2 * units), f32),
            jax.ShapeDtypeStruct((count, 2 * units), bf16),
            jax.ShapeDtypeStruct((count, D), bf16),
            jax.ShapeDtypeStruct((count, D), bf16),
            jax.ShapeDtypeStruct((count, D), bf16),
        ],
        scratch_shapes=[
            pltpu.VMEM((count, D), bf16),
            pltpu.VMEM((count, D), bf16),
            pltpu.SemaphoreType.DMA((7,)),
            pltpu.SemaphoreType.DMA((7,)),
            pltpu.SemaphoreType.DMA((2,)),
        ],
        compiler_params=pltpu.CompilerParams(vmem_limit_bytes=56 * 1024 * 1024),
    )(gate, limit, unit, up_mine, up_other, *feed, *upstream)


def mixed_back_kernel(weight_ref, *others):
    pieces, (grad_ref, all_ref, whole_ref, sem, out_sem) = others[:7], others[7:]
    copies = copies_in(pieces, whole_ref, sem)
    copy_out = pltpu.make_async_copy(whole_ref, all_ref, out_sem)
    for copy in copies:
        copy.start()
    for copy in copies:
        copy.wait()
    copy_out.start()
    grad_ref[...] = contract_last(whole_ref[...], weight_ref[...]).astype(bf16)
    copy_out.wait()


def mixed_back(weight, pieces):
    count = sum(piece.shape[0] for piece in pieces)
    return pl.pallas_call(
        mixed_back_kernel,
        in_specs=[pl.BlockSpec(memory_space=pltpu.VMEM)]
        + [pl.BlockSpec(memory_space=pl.ANY)] * len(pieces),
        out_specs=[pl.BlockSpec(memory_space=pltpu.VMEM), pl.BlockSpec(memory_space=pl.ANY)],
        out_shape=[
            jax.ShapeDtypeStruct((count, weight.shape[0]), bf16),
            jax.ShapeDtypeStruct((count, D), bf16),
        ],
        scratch_shapes=[
            pltpu.VMEM((count, D), bf16),
            pltpu.SemaphoreType.DMA((len(pieces),)),
            pltpu.SemaphoreType.DMA,
        ],
        compiler_params=pltpu.CompilerParams(vmem_limit_bytes=48 * 1024 * 1024),
    )(weight, *pieces)


def lower_kernel(
    half,
    grad_ref,
    rectified_ref,
    down_mine_ref,
    down_other_ref,
    up_mine_ref,
    up_other_ref,
    lifted_ref,
    input_ref,
    kept_ref,
):
    step = pl.program_id(0)
    count, block = rectified_ref.shape
    units = half * block

    @pl.when(step < 2 * half)
    def _():
        columns = pl.ds(pl.multiple_of(step * block, block), block)

        def body(down_ref):
            for at in narrower(block):
                grad = contract_last(grad_ref[...], down_ref[at, :])
                lifted_ref[:, at] = (grad * 2.0 * rectified_ref[:, at]).astype(bf16)

        of_two(step, half, body, down_mine_ref, down_other_ref)
        kept_ref[:, columns] = lifted_ref[...]

    @pl.when(step >= 2 * half)
    def _():
        for at in narrower(input_ref.shape[1]):
            input_ref[:, at] = (
                contract_last(kept_ref[:, :units], up_mine_ref[at, :])
                + contract_last(kept_ref[:, units:], up_other_ref[at, :])
            ).astype(bf16)


def lower(grad, rectified, down_mine, down_other, up_mine, up_other):
    count, units = grad.shape[0], up_mine.shape[1]
    block = min(BLOCK, units)
    half = units // block
    first, second = 2 * half, D // BLOCK
    once = pl.Buffered(1)
    return pl.pallas_call(
        functools.partial(lower_kernel, half),
        grid=(first + second,),
        in_specs=[
            pl.BlockSpec((count, D), lambda s: (0, 0), pipeline_mode=once),
            pl.BlockSpec((count, block), lambda s: (0, jnp.minimum(s, first - 1))),
            pl.BlockSpec((block, D), lambda s: (jnp.minimum(s, half - 1), 0)),
            pl.BlockSpec((block, D), lambda s: (jnp.clip(s - half, 0, half - 1), 0)),
            pl.BlockSpec((BLOCK, units), lambda s: (jnp.maximum(s - first, 0), 0)),
            pl.BlockSpec((BLOCK, units), lambda s: (jnp.maximum(s - first, 0), 0)),
        ],
        out_specs=[
            pl.BlockSpec((count, block), lambda s: (0, jnp.minimum(s, first - 1))),
            pl.BlockSpec((count, BLOCK), lambda s: (0, jnp.maximum(s - first, 0))),
        ],
        out_shape=[
            jax.ShapeDtypeStruct((count, 2 * units), bf16),
            jax.ShapeDtypeStruct((count, D), bf16),
        ],
        scratch_shapes=[pltpu.VMEM((count, 2 * units), bf16)],
        compiler_params=pltpu.CompilerParams(vmem_limit_bytes=56 * 1024 * 1024),
    )(grad, rectified, down_mine, down_other, up_mine, up_other)


def branch_kernel(activated_ref, upstream_ref, mine_ref, other_ref, branch_ref, part_ref):
    units = mine_ref.shape[0]
    total = None
    for at in narrower(branch_ref.shape[1]):
        branch = dot_plain(activated_ref[:, :units], mine_ref[:, at]) + dot_plain(
            activated_ref[:, units:], other_ref[:, at]
        )
        branch_ref[:, at] = branch.astype(bf16)
        part = jnp.sum(branch * upstream_ref[:, at].astype(f32), axis=1, keepdims=True)
        total = part if total is None else total + part

    @pl.when(pl.program_id(0) == 0)
    def _():
        part_ref[...] = total

    @pl.when(pl.program_id(0) > 0)
    def _():
        part_ref[...] += total


def branch(activated, upstream, down_mine, down_other):
    count, units = activated.shape[0], down_mine.shape[0]
    once = pl.Buffered(1)
    return pl.pallas_call(
        branch_kernel,
        grid=(D // BLOCK,),
        in_specs=[
            pl.BlockSpec((count, 2 * units), lambda s: (0, 0), pipeline_mode=once),
            pl.BlockSpec((count, BLOCK), lambda s: (0, s)),
            pl.BlockSpec((units, BLOCK), lambda s: (0, s)),
            pl.BlockSpec((units, BLOCK), lambda s: (0, s)),
        ],
        out_specs=[
            pl.BlockSpec((count, BLOCK), lambda s: (0, s)),
            pl.BlockSpec((count, 1), lambda s: (0, 0)),
        ],
        out_shape=[
            jax.ShapeDtypeStruct((count, D), bf16),
            jax.ShapeDtypeStruct((count, 1), f32),
        ],
        compiler_params=pltpu.CompilerParams(vmem_limit_bytes=56 * 1024 * 1024),
    )(activated, upstream, down_mine, down_other)


def local(
    planes,
    tokens,
    documents,
    head_level,
    width_level,
    mixer_gain,
    mixer_bias,
    input_weight,
    output_weight,
    mixer_router,
    feed_gain,
    feed_bias,
    up_weight,
    down_weight,
    feed_router,
    cotangent,
):
    rows = tokens.shape[0]
    seq_rows = documents.shape[1]
    weight_rows = input_weight.shape[0]
    unit_rows = down_weight.shape[0]
    at_core = lax.axis_index("c")
    chip = lax.axis_index("x") * 2 + lax.axis_index("y")
    at_plane = chip * 2 + at_core
    quarter = at_plane % (seq_rows // rows)
    place = jnp.stack([quarter, 2 * at_core]).astype(jnp.int32)

    def pieces(values):
        return [values[at : at + rows] for at in range(0, values.shape[0], rows)]

    def both_cores(mine, other):
        return (mine.astype(f32) + flip(other, "c").astype(f32)).astype(bf16)

    levels = jnp.concatenate(
        [head_level.reshape(2, rows // 2), width_level.reshape(2, rows // 2)], axis=1
    )
    levels = levels.astype(f32)
    levels = gather_small(levels)
    plane_docs = jnp.concatenate([documents, flip(documents, "x")], axis=0)
    starts = jnp.sum(
        (plane_docs[:, None, :] < plane_docs[:, :, None]).astype(jnp.int32), axis=2
    ).reshape(2 * seq_rows, 1)
    level_range = jnp.arange(OPTIONS)
    head_counts = jnp.sum((head_level[:, None] == level_range[None, :]).astype(f32), axis=0)
    width_counts = jnp.sum((width_level[:, None] == level_range[None, :]).astype(f32), axis=0)

    output_blocks = [output_weight]
    if planes == 4:
        output_blocks += [
            lax.ppermute(output_weight, "z", [(i, i ^ d) for i in range(planes)])
            for d in range(1, planes)
        ]
    input_first = swap_plane(deal(input_weight, attention_columns()))
    weights = [lax.all_gather(input_first[:, : 3 * HD], "z", axis=0, tiled=True)]
    token_values = tokens.astype(f32)
    mixer_hidden, mixer_normed, mixer_scale = normalize(token_values, mixer_gain, mixer_bias)
    mixer_gate, mixer_probs, mixer_chosen = route(mixer_hidden, mixer_router, head_level)
    mixer_pieces = gather_eight(mixer_hidden.astype(bf16))
    (
        mixer_pieces[1:5],
        input_second,
        output_blocks,
        up_weight,
        cotangent_sent,
        levels,
        starts,
    ) = lax.optimization_barrier(
        (
            mixer_pieces[1:5],
            input_first[:, 3 * HD :],
            output_blocks,
            up_weight,
            cotangent,
            levels,
            starts,
        )
    )
    weights.append(lax.all_gather(input_second, "z", axis=0, tiled=True))
    output_share = share_heads(output_blocks)
    width_all = levels[:, :, rows // 2 :].reshape(4 * rows)
    limit = (width_all[:, None].astype(jnp.int32) + 1) * (FF // OPTIONS)
    head_all = levels[:, :, : rows // 2].reshape(4, rows)
    head_all = jnp.concatenate([head_all, flip(head_all, "c")], axis=0)
    head_all = head_all.reshape(2, 2, 2 * rows, 1)
    up_first = swap_plane(deal(up_weight, unit_columns(planes, unit_rows)))
    weights[1], up_first = lax.optimization_barrier((weights[1], up_first))
    up_mine = lax.all_gather(up_first, "z", axis=0, tiled=True)
    down_mine = lax.all_gather(after(down_weight, up_first), "z", axis=0, tiled=True)
    upstream_pieces = gather_four(cotangent_sent)

    cos_table, sin_table = rope_tables(jnp.arange(seq_rows).astype(f32))
    attending = functools.partial(attend, place, starts, head_all, cos_table, sin_table)
    rotated_0, mixed_0, mixer_all = attending(weights[0], mixer_pieces, rows, 0)
    weights[1], mixed_0, upstream_pieces[1:5] = lax.optimization_barrier(
        (weights[1], mixed_0, upstream_pieces[1:5])
    )
    rotated_1, mixed_1, _ = attending(weights[1], mixer_pieces, rows, 1)
    mixed = [m.reshape(2, 4 * rows, HD) for m in (mixed_0, mixed_1)]
    mixed_all = jnp.concatenate(
        [m[0] for m in mixed] + [flip(m[1], "c") for m in mixed], axis=1
    )
    mixed_all, upstream_pieces[5:] = lax.optimization_barrier((mixed_all, upstream_pieces[5:]))
    mixer_branch = scatter_four(pieces(dot_plain(mixed_all, output_share).astype(bf16)))
    middle = token_values + mixer_gate[:, None] * mixer_branch
    feed_hidden, feed_normed, feed_scale = normalize(middle, feed_gain, feed_bias)
    feed_gate, feed_probs, feed_chosen = route(feed_hidden, feed_router, width_level)
    upstream = cotangent.astype(f32)

    up_mine, feed_low = lax.optimization_barrier((up_mine, feed_hidden.astype(bf16)))
    up_other = flip(up_mine, "c")
    feed_pieces = gather_four(feed_low)
    gate_all = gather_small(feed_gate.reshape(2, rows // 2)).reshape(4 * rows, 1)
    units = planes * unit_rows
    unit = jnp.arange(units, dtype=jnp.int32)
    unit = jnp.concatenate(
        [
            (unit // unit_rows * GROUP + share) * unit_rows + unit % unit_rows
            for share in (at_plane, at_plane ^ 1)
        ]
    )
    rectified, activated, grad_branch_all, feed_all, upstream_all = lift(
        gate_all, limit, unit[None, :], up_mine, up_other, feed_pieces, upstream_pieces
    )
    down_part_other = contract_first(activated[:, units:], grad_branch_all).astype(bf16)
    down_part = both_cores(
        contract_first(activated[:, :units], grad_branch_all), down_part_other
    )
    down_mine, down_part_other = lax.optimization_barrier((down_mine, down_part_other))
    down_other = flip(down_mine, "c")
    down_sum = lax.psum_scatter(down_part, "z", scatter_dimension=0, tiled=True)
    lifted, input_pieces = lower(
        grad_branch_all, rectified, down_mine, down_other, up_mine, up_other
    )
    activated, input_pieces = lax.optimization_barrier((activated, input_pieces))
    input_pieces = pieces(input_pieces)
    input_sent = scatter_send(input_pieces)
    branch_pieces, gate_part = branch(activated, upstream_all, down_mine, down_other)
    lifted, gate_part, input_sent = lax.optimization_barrier((lifted, gate_part, input_sent))
    grad_feed_gate = sum_small(gate_part.reshape(4, 2, rows // 2)).reshape(rows)
    up_part_other = contract_first(feed_all, lifted[:, units:]).astype(bf16)
    up_part = both_cores(contract_first(feed_all, lifted[:, :units]), up_part_other)
    grad_feed_input = scatter_end(input_pieces, input_sent)

    feed_router_term, grad_feed_routed = route_back(
        grad_feed_gate, feed_probs, feed_chosen, feed_hidden, feed_router
    )
    grad_middle_norm, feed_gain_term, feed_bias_term = normalize_back(
        grad_feed_input + grad_feed_routed, feed_normed, feed_scale, feed_gain
    )
    grad_middle = upstream + grad_middle_norm
    grad_mixer_gate = jnp.sum(mixer_branch * grad_middle, axis=1)
    grad_mixer_branch = (mixer_gate[:, None] * grad_middle).astype(bf16)
    grad_mixer_branch, down_sum, up_part = lax.optimization_barrier(
        (grad_mixer_branch, down_sum, up_part)
    )
    up_sum = lax.psum_scatter(up_part, "z", scatter_dimension=0, tiled=True)
    grad_attended, grad_mixer_all = mixed_back(output_share, gather_four(grad_mixer_branch))
    grad_attended = jnp.concatenate(
        [grad_attended[:, :SHARE], flip(grad_attended[:, SHARE:], "c")], axis=0
    )

    branch_pieces, grad_attended = lax.optimization_barrier((branch_pieces, grad_attended))
    branch_pieces = pieces(branch_pieces)
    branch_sent = scatter_send(branch_pieces)
    output_part = contract_first(mixed_all, grad_mixer_all).astype(bf16)
    grad_projected, mixer_pieces = attend_back(
        place,
        starts,
        head_all,
        cos_table,
        sin_table,
        (rotated_0, rotated_1),
        grad_attended,
        weights,
        rows,
    )
    grad_projected, up_sum, branch_sent = lax.optimization_barrier(
        (grad_projected, up_sum, branch_sent)
    )
    feed_branch = scatter_end(branch_pieces, branch_sent)
    input_part = contract_first(mixer_all, grad_projected).astype(bf16)
    input_sum = lax.psum_scatter(input_part, "z", scatter_dimension=0, tiled=True)
    mixer_pieces, feed_branch = lax.optimization_barrier(
        (add_cores(pieces(mixer_pieces)), feed_branch)
    )
    outputs = (middle + feed_gate[:, None] * feed_branch).astype(bf16)
    grad_mixer_input = scatter_four(mixer_pieces)
    input_sum, output_part = lax.optimization_barrier((input_sum, output_part))
    grad_output_weight = sum_heads(output_part, planes, weight_rows).astype(f32)
    grad_mixer_input, up_sum = lax.optimization_barrier((grad_mixer_input, up_sum))
    up_back = swap_plane(up_sum)

    mixer_router_term, grad_mixer_routed = route_back(
        grad_mixer_gate, mixer_probs, mixer_chosen, mixer_hidden, mixer_router
    )
    grad_token_norm, mixer_gain_term, mixer_bias_term = normalize_back(
        grad_mixer_input + grad_mixer_routed, mixer_normed, mixer_scale, mixer_gain
    )
    grad_tokens = grad_middle + grad_token_norm
    counts = jnp.pad(jnp.concatenate([head_counts, width_counts]), (0, D - 2 * OPTIONS))
    rows_of = [mixer_gain_term, mixer_bias_term, feed_gain_term, feed_bias_term, counts]
    sums, input_back = sum_everywhere(
        jnp.concatenate([jnp.stack(rows_of), mixer_router_term, feed_router_term], axis=0),
        planes,
        swap_plane(input_sum),
    )
    grad_down_weight = down_sum.astype(f32)
    grad_up_weight = undeal(up_back, unit_columns(planes, unit_rows))
    grad_input_weight = undeal(input_back, attention_columns())
    return (
        outputs,
        grad_tokens,
        sums[0],
        sums[1],
        grad_input_weight,
        grad_output_weight,
        sums[5:9].T,
        sums[2],
        sums[3],
        grad_up_weight,
        grad_down_weight,
        sums[9:13].T,
        sums[4, : 2 * OPTIONS].reshape(2, OPTIONS),
    )


def solution(mesh):
    wide, narrow = mesh.shape["wide"], mesh.shape["narrow"]
    planes = wide // 2
    inner = Mesh(mesh.devices.reshape(planes, 2, narrow // 2, 2), ALL)
    rowwise = P(ALL, None)
    in_specs = (
        rowwise,
        P(("z", "x"), None),
        P(ALL),
        P(ALL),
        P(),
        P(),
        rowwise,
        rowwise,
        P(),
        P(),
        P(),
        rowwise,
        rowwise,
        P(),
        rowwise,
    )
    out_specs = (
        rowwise,
        rowwise,
        P(),
        P(),
        rowwise,
        rowwise,
        P(),
        P(),
        P(),
        rowwise,
        rowwise,
        P(),
        P(),
    )
    return jax.shard_map(
        functools.partial(local, planes),
        mesh=inner,
        in_specs=in_specs,
        out_specs=out_specs,
        check_vma=False,
    )
```

```python
import functools

import jax
import jax.numpy as jnp
from jax import lax
from jax.experimental import pallas as pl
from jax.experimental.pallas import tpu as pltpu
from jax.sharding import Mesh, PartitionSpec as P

D = 2048
H = 16
HD = 128
FF = 8192
OPTIONS = 4
LONGEST = 512

PLANE = ("x", "y", "c")
ALL = ("z", "x", "y", "c")
GROUP = 8
SHARE = D // GROUP

highest = lax.Precision.HIGHEST
epsilon = 1e-05
masked_score = -1e30
f32 = jnp.float32
bf16 = jnp.bfloat16


def normalize(values, gain_vec, shift_vec):
    centre = values - jnp.mean(values, axis=1, keepdims=True)
    inv_scale = lax.rsqrt(jnp.mean(centre * centre, axis=1, keepdims=True) + epsilon)
    normed = centre * inv_scale
    return (normed * gain_vec + shift_vec, normed, inv_scale)


def normalize_back(grad_hidden, normed, inv_scale, gain_vec):
    grad_normed = grad_hidden * gain_vec
    inner = (
        grad_normed
        - jnp.mean(grad_normed, axis=1, keepdims=True)
        - normed * jnp.mean(grad_normed * normed, axis=1, keepdims=True)
    )
    return (inv_scale * inner, jnp.sum(grad_hidden * normed, axis=0), jnp.sum(grad_hidden, axis=0))


def route(hidden, router, picked):
    logits = jnp.dot(hidden, router, precision=highest)
    shifted = jnp.exp(logits - jnp.max(logits, axis=1, keepdims=True))
    prob_rows = shifted / jnp.sum(shifted, axis=1, keepdims=True)
    chosen = (jnp.arange(router.shape[1])[None, :] == picked[:, None]).astype(f32)
    return (router.shape[1] * jnp.sum(prob_rows * chosen, axis=1), prob_rows, chosen)


def route_back(grad_gate, prob_rows, chosen, hidden, router):
    grad_prob = router.shape[1] * grad_gate[:, None] * chosen
    grad_logits = prob_rows * (grad_prob - jnp.sum(grad_prob * prob_rows, axis=1, keepdims=True))
    grad_router = lax.dot_general(
        grad_logits, hidden, (((0,), (0,)), ((), ())), precision=highest
    )
    grad_hidden = jnp.dot(grad_logits, router.T, precision=highest)
    return (grad_router, grad_hidden)


def rope_tables(positions):
    half_width = HD // 2
    exponent = jnp.arange(half_width).astype(f32) * (-2.0 / HD)
    frequency = jnp.power(10000.0, exponent)
    angles = positions[:, None] * frequency[None, :]
    cos_half, sin_half = jnp.cos(angles), jnp.sin(angles)
    return (
        jnp.concatenate([cos_half, cos_half], axis=1),
        jnp.concatenate([-sin_half, sin_half], axis=1),
    )


def dot_plain(left, right):
    return jnp.dot(left, right, preferred_element_type=f32)


def contract_last(left, right):
    return lax.dot_general(left, right, (((1,), (1,)), ((), ())), preferred_element_type=f32)


def contract_first(left, right):
    return lax.dot_general(left, right, (((0,), (0,)), ((), ())), preferred_element_type=f32)


def flip(values, axis):
    return lax.ppermute(values, axis, [(0, 1), (1, 0)])


def gather_four(values):
    half = values.shape[0] // 2
    top, bottom = values[:half], values[half:]
    y_top, x_bottom = flip(top, "y"), flip(bottom, "x")
    y_bottom, x_top = flip(bottom, "y"), flip(top, "x")
    return [values, y_top, y_bottom, x_top, x_bottom, flip(y_top, "x"), flip(x_bottom, "y")]


def gather_eight(values):
    chunks = gather_four(values)
    return chunks + [flip(chunk, "c") for chunk in chunks]


def copies_in(pieces, whole, sem):
    copies, at = [], 0
    for i, piece in enumerate(pieces):
        count = piece.shape[0]
        copies.append(pltpu.make_async_copy(piece, whole.at[at : at + count, :], sem.at[i]))
        at += count
    return copies


def scatter_send(parts):
    half = parts[0].shape[0] // 2
    by_x, by_y = flip(parts[3][:half], "x"), flip(parts[3][half:], "y")
    x_top, y_bottom = flip(parts[2][:half], "x"), flip(parts[1][half:], "y")
    return by_x, by_y, x_top, y_bottom


def scatter_end(parts, sent):
    half = parts[0].shape[0] // 2
    by_x, by_y, x_top, y_bottom = sent
    y_top = flip((parts[1][:half].astype(f32) + by_x.astype(f32)).astype(bf16), "y")
    x_bottom = flip((parts[2][half:].astype(f32) + by_y.astype(f32)).astype(bf16), "x")
    own = parts[0].astype(f32)
    return jnp.concatenate(
        [
            own[:half] + x_top.astype(f32) + y_top.astype(f32),
            own[half:] + x_bottom.astype(f32) + y_bottom.astype(f32),
        ],
        axis=0,
    )


def scatter_four(parts):
    return scatter_end(parts, scatter_send(parts))


def add_cores(parts):
    other = [flip(part, "c") for part in parts[4:]]
    return [(a.astype(f32) + b.astype(f32)).astype(bf16) for a, b in zip(parts[:4], other)]


def send_four(values, d):
    return lax.ppermute(values, ("x", "y"), [(i, i ^ d) for i in range(4)])


def gather_small(values):
    return jnp.stack([values] + [send_four(values, d) for d in range(1, 4)])


def sum_small(values):
    return values[0] + sum(send_four(values[d], d) for d in range(1, 4))


def sum_everywhere(values, planes, before_last):
    for axis in ("c", "y", "x"):
        values = values + flip(values, axis)
    if planes & (planes - 1):
        return lax.psum(values, "z"), before_last
    step = 1
    while step < planes:
        if 2 * step == planes:
            values, before_last = lax.optimization_barrier((values, before_last))
        values = values + lax.ppermute(values, "z", [(i, i ^ step) for i in range(planes)])
        step *= 2
    return values, before_last


def after(values, *others):
    return lax.optimization_barrier((values, *others))[0]


def head_numbers():
    chip = lax.axis_index("x") * 2 + lax.axis_index("y")
    return [chip + 4 * (2 * lax.axis_index("c") + e) for e in range(2)]


def by_core(mine, other, axis):
    return jnp.where(
        lax.axis_index("c") == 0,
        jnp.concatenate([mine, other], axis=axis),
        jnp.concatenate([other, mine], axis=axis),
    )


def share_heads(blocks):
    weight_rows = blocks[0].shape[0]
    if len(blocks) == 1 or 2 * weight_rows != HD:
        full = lax.all_gather(blocks[0], ALL, axis=0, tiled=True)
        mine = [lax.dynamic_slice_in_dim(full, h * HD, HD, 0) for h in head_numbers()]
        mine = jnp.concatenate(mine, axis=0)
        return jnp.concatenate([mine, flip(mine, "c")], axis=0)
    halves = jnp.zeros((len(blocks), 1, weight_rows, D), bf16)
    for d, block in enumerate(blocks):
        at = lax.axis_index("z") ^ d
        halves = lax.dynamic_update_slice(halves, block[None, None], (at, 0, 0, 0))
    heads = by_core(halves, flip(halves, "c"), 1)
    core = lax.axis_index("c")
    return jnp.concatenate(
        [
            lax.dynamic_slice_in_dim(heads, 2 * core, 2, 0),
            lax.dynamic_slice_in_dim(heads, 2 - 2 * core, 2, 0),
        ],
        axis=0,
    ).reshape(2 * SHARE, D)


def sum_heads(part, planes, weight_rows):
    if 2 * weight_rows != HD:
        mine = part[:SHARE] + flip(part[SHARE:], "c")
        full = jnp.zeros((D, D), part.dtype)
        for e, h in enumerate(head_numbers()):
            full = lax.dynamic_update_slice(full, mine[e * HD : (e + 1) * HD], (h * HD, 0))
        return lax.psum_scatter(full, ALL, scatter_dimension=0, tiled=True)
    core = lax.axis_index("c")
    halves = part.reshape(4, 2, weight_rows, D)
    mine = lax.dynamic_slice_in_dim(halves, core, 1, 1)[:, 0]
    other = flip(lax.dynamic_slice_in_dim(halves, 1 - core, 1, 1)[:, 0], "c")
    first = (mine[:2].astype(f32) + other[2:].astype(f32)).astype(bf16)
    second = (mine[2:].astype(f32) + other[:2].astype(f32)).astype(bf16)
    return lax.psum_scatter(
        by_core(first, second, 0).reshape(planes * weight_rows, D),
        "z",
        scatter_dimension=0,
        tiled=True,
    )


def attention_columns():
    return [
        (part * D + (p // 2 + 4 * (2 * (p % 2) + e)) * HD, HD, p, (e * 3 + part) * HD)
        for p in range(GROUP)
        for part in range(3)
        for e in range(2)
    ]


def unit_columns(planes, unit_rows):
    return [
        ((k * GROUP + p) * unit_rows, unit_rows, p, k * unit_rows)
        for p in range(GROUP)
        for k in range(planes)
    ]


def deal_kernel(moves, whole_ref, dealt_ref):
    for first, width, p, at in moves:
        dealt_ref[p, :, at : at + width] = whole_ref[:, first : first + width]


def deal(whole, moves):
    rows, columns = whole.shape
    if any(width % 128 for _, width, _, _ in moves):
        parts = [[] for _ in range(GROUP)]
        for first, width, p, _ in moves:
            parts[p].append(whole[:, first : first + width])
        return jnp.concatenate([jnp.concatenate(part, axis=1) for part in parts], axis=0)
    dealt = pl.pallas_call(
        functools.partial(deal_kernel, moves),
        out_shape=jax.ShapeDtypeStruct((GROUP, rows, columns // GROUP), whole.dtype),
    )(whole)
    return dealt.reshape(GROUP * rows, columns // GROUP)


def undeal_kernel(moves, dealt_ref, whole_ref):
    for first, width, p, at in moves:
        whole_ref[:, first : first + width] = dealt_ref[p, :, at : at + width].astype(f32)


def undeal(dealt, moves):
    rows, columns = dealt.shape[0] // GROUP, dealt.shape[1] * GROUP
    dealt = dealt.reshape(GROUP, rows, columns // GROUP)
    if any(width % 128 for _, width, _, _ in moves):
        return jnp.concatenate(
            [dealt[p, :, at : at + width] for _, width, p, at in sorted(moves)], axis=1
        ).astype(f32)
    return pl.pallas_call(
        functools.partial(undeal_kernel, moves),
        out_shape=jax.ShapeDtypeStruct((rows, columns), f32),
    )(dealt)


def swap_plane(values):
    return lax.all_to_all(values, PLANE, 0, 0, tiled=True)


def chunk_at(block, quarter, rows):
    differs = block ^ quarter
    return differs % 2, pl.ds(pl.multiple_of(differs // 2 * rows, rows), rows)


def key_blocks(block, rows):
    return range(max(0, (block * rows - (LONGEST - 1)) // rows), block + 1)


def visible(start_col, block, key_block, rows):
    key_pos = key_block * rows + lax.broadcasted_iota(jnp.int32, (rows, rows), 1)
    seen = key_pos >= start_col
    if key_block == block:
        seen &= key_pos <= block * rows + lax.broadcasted_iota(jnp.int32, (rows, rows), 0)
    return seen


def softmax_blocks(query, rot_ref, start_col, block, rows, key_at):
    scores = []
    for key_block in key_blocks(block, rows):
        keys = rot_ref[key_block * rows : (key_block + 1) * rows, key_at : key_at + HD]
        piece = contract_last(query, keys) * HD ** (-0.5)
        scores.append(
            jnp.where(visible(start_col, block, key_block, rows), piece, masked_score)
        )
    top = functools.reduce(
        jnp.maximum, [jnp.max(piece, axis=1, keepdims=True) for piece in scores]
    )
    weights = [jnp.exp(piece - top) for piece in scores]
    total = functools.reduce(
        jnp.add, [jnp.sum(piece, axis=1, keepdims=True) for piece in weights]
    )
    inverse = 1.0 / total
    return [piece * inverse for piece in weights]


def attend_kernel(
    rows,
    blocks,
    head,
    place_ref,
    start_ref,
    level_ref,
    cos_ref,
    sin_ref,
    weight_ref,
    *others,
):
    pieces, others = others[:-6], others[-6:]
    rot_ref, out_ref, all_ref, hidden_ref, sem, out_sem = others
    quarter = place_ref[0]
    level_least = place_ref[1]
    sequence = pl.program_id(0)
    copies = copies_in(pieces, hidden_ref, sem)
    copy_out = pltpu.make_async_copy(hidden_ref, all_ref, out_sem)
    first = [copies[i] for i in (0, 1, 2, 7, 8, 9)]
    second = [copies[i] for i in (3, 4, 5, 6, 10, 11, 12, 13)]

    @pl.when(sequence == 0)
    def _():
        for copy in first + second:
            copy.start()
        for copy in first:
            copy.wait()

    @pl.when(sequence == 1)
    def _():
        for copy in second:
            copy.wait()
        copy_out.start()

    for block in range(blocks):
        here = slice(block * rows, (block + 1) * rows)
        other, there = chunk_at(block, quarter, rows)
        cos_rows, sin_rows = cos_ref[here, :], sin_ref[here, :]
        at = (other * 4 + sequence * 2 + (block ^ quarter) // 2) * rows
        hidden = hidden_ref[pl.ds(pl.multiple_of(at, rows), rows), :]
        projected = dot_plain(hidden, weight_ref[...])
        for col in range(0, 2 * HD, HD):
            piece = projected[:, col : col + HD]
            turned = piece * cos_rows + pltpu.roll(piece, HD // 2, 1) * sin_rows
            rot_ref[here, col : col + HD] = turned.astype(bf16)
        rot_ref[here, 2 * HD :] = projected[:, 2 * HD :].astype(bf16)
    for block in range(blocks):
        here = slice(block * rows, (block + 1) * rows)
        other, there = chunk_at(block, quarter, rows)
        query = rot_ref[here, :HD]
        probs = softmax_blocks(query, rot_ref, start_ref[here, :], block, rows, HD)
        total = None
        for key_block, piece in zip(key_blocks(block, rows), probs):
            values = rot_ref[key_block * rows : (key_block + 1) * rows, 2 * HD :]
            term = dot_plain(piece.astype(bf16), values)
            total = term if total is None else total + term
        kept = level_ref[other, there, :] >= level_least + head
        out_ref[other, there, :] = jnp.where(kept, total, 0.0).astype(bf16)

    @pl.when(sequence == 1)
    def _():
        copy_out.wait()


def attend_back_kernel(
    rows,
    blocks,
    place_ref,
    start_ref,
    level_ref,
    cos_ref,
    sin_ref,
    rot_refs_0,
    rot_refs_1,
    grad_ref,
    weight_0,
    weight_1,
    out_ref,
    hidden_ref,
    key_acc,
    value_acc,
):
    quarter = place_ref[0]
    level_least = place_ref[1]
    scale = HD ** (-0.5)

    def turn_back(piece, here):
        return piece * cos_ref[here, :] - pltpu.roll(piece, HD // 2, 1) * sin_ref[here, :]

    for head, rot_ref in ((0, rot_refs_0), (HD, rot_refs_1)):
        key_at, value_at = HD, 2 * HD
        out_at = head * 3
        key_acc[...] = jnp.zeros_like(key_acc)
        value_acc[...] = jnp.zeros_like(value_acc)
        for block in range(blocks):
            here = slice(block * rows, (block + 1) * rows)
            other, there = chunk_at(block, quarter, rows)
            query = rot_ref[here, :HD]
            kept = level_ref[other, there, :] >= level_least + head // HD
            grad = jnp.where(kept, grad_ref[other, there, head : head + HD], 0.0).astype(bf16)
            probs = softmax_blocks(query, rot_ref, start_ref[here, :], block, rows, key_at)
            grad_probs, inner = [], None
            for key_block, piece in zip(key_blocks(block, rows), probs):
                keys_at = slice(key_block * rows, (key_block + 1) * rows)
                grad_piece = contract_last(grad, rot_ref[keys_at, value_at : value_at + HD])
                grad_probs.append(grad_piece)
                term = jnp.sum(grad_piece * piece, axis=1, keepdims=True)
                inner = term if inner is None else inner + term
            query_grad = None
            for key_block, piece, grad_piece in zip(key_blocks(block, rows), probs, grad_probs):
                keys_at = slice(key_block * rows, (key_block + 1) * rows)
                grad_scores = (piece * (grad_piece - inner)).astype(bf16)
                term = dot_plain(grad_scores, rot_ref[keys_at, key_at : key_at + HD])
                query_grad = term if query_grad is None else query_grad + term
                key_acc[keys_at, :] += contract_first(grad_scores, query)
                value_acc[keys_at, :] += contract_first(piece.astype(bf16), grad)
            out_ref[other, there, out_at : out_at + HD] = turn_back(query_grad * scale, here).astype(bf16)
        for block in range(blocks):
            here = slice(block * rows, (block + 1) * rows)
            other, there = chunk_at(block, quarter, rows)
            out_ref[other, there, out_at + HD : out_at + 2 * HD] = turn_back(
                key_acc[here, :] * scale, here
            ).astype(bf16)
            out_ref[other, there, out_at + 2 * HD : out_at + 3 * HD] = value_acc[
                here, :
            ].astype(bf16)
    for block in range(blocks):
        other, there = chunk_at(block, quarter, rows)
        hidden_ref[other, there, :] = (
            contract_last(out_ref[other, there, : 3 * HD], weight_0[...])
            + contract_last(out_ref[other, there, 3 * HD :], weight_1[...])
        ).astype(bf16)


def chunked(seq_rows, columns):
    return pl.BlockSpec((2, None, seq_rows // 2, columns), lambda s, place: (0, s, 0, 0))


def attend(place, starts, levels, cos_table, sin_table, weight, pieces, rows, head):
    seq_rows = cos_table.shape[0]
    body = functools.partial(attend_kernel, rows, seq_rows // rows, head)
    return pl.pallas_call(
        body,
        grid_spec=pltpu.PrefetchScalarGridSpec(
            num_scalar_prefetch=1,
            grid=(2,),
            in_specs=[
                pl.BlockSpec((seq_rows, 1), lambda s, place: (s, 0)),
                chunked(seq_rows, 1),
                pl.BlockSpec((seq_rows, HD), lambda s, place: (0, 0)),
                pl.BlockSpec((seq_rows, HD), lambda s, place: (0, 0)),
                pl.BlockSpec((D, 3 * HD), lambda s, place: (0, 0)),
            ]
            + [pl.BlockSpec(memory_space=pl.ANY)] * len(pieces),
            out_specs=[
                pl.BlockSpec((seq_rows, 3 * HD), lambda s, place: (s, 0)),
                chunked(seq_rows, HD),
                pl.BlockSpec(memory_space=pl.ANY),
            ],
            scratch_shapes=[
                pltpu.VMEM((2 * seq_rows, D), bf16),
                pltpu.SemaphoreType.DMA((len(pieces),)),
                pltpu.SemaphoreType.DMA,
            ],
        ),
        out_shape=[
            jax.ShapeDtypeStruct((2 * seq_rows, 3 * HD), bf16),
            jax.ShapeDtypeStruct((2, 2, seq_rows // 2, HD), bf16),
            jax.ShapeDtypeStruct((2 * seq_rows, D), bf16),
        ],
        compiler_params=pltpu.CompilerParams(vmem_limit_bytes=48 * 1024 * 1024),
    )(
        place,
        starts,
        levels,
        cos_table,
        sin_table,
        weight,
        *pieces,
    )


def attend_back(place, starts, levels, cos_table, sin_table, rotated, grad, weights, rows):
    seq_rows = cos_table.shape[0]
    body = functools.partial(attend_back_kernel, rows, seq_rows // rows)
    grad_projected, grad_hidden = pl.pallas_call(
        body,
        grid_spec=pltpu.PrefetchScalarGridSpec(
            num_scalar_prefetch=1,
            grid=(2,),
            in_specs=[
                pl.BlockSpec((seq_rows, 1), lambda s, place: (s, 0)),
                chunked(seq_rows, 1),
                pl.BlockSpec((seq_rows, HD), lambda s, place: (0, 0)),
                pl.BlockSpec((seq_rows, HD), lambda s, place: (0, 0)),
                pl.BlockSpec((seq_rows, 3 * HD), lambda s, place: (s, 0)),
                pl.BlockSpec((seq_rows, 3 * HD), lambda s, place: (s, 0)),
                chunked(seq_rows, SHARE),
                pl.BlockSpec((D, 3 * HD), lambda s, place: (0, 0)),
                pl.BlockSpec((D, 3 * HD), lambda s, place: (0, 0)),
            ],
            out_specs=[chunked(seq_rows, 3 * SHARE), chunked(seq_rows, D)],
            scratch_shapes=[pltpu.VMEM((seq_rows, HD), f32), pltpu.VMEM((seq_rows, HD), f32)],
        ),
        out_shape=[
            jax.ShapeDtypeStruct((2, 2, seq_rows // 2, 3 * SHARE), bf16),
            jax.ShapeDtypeStruct((2, 2, seq_rows // 2, D), bf16),
        ],
        compiler_params=pltpu.CompilerParams(vmem_limit_bytes=48 * 1024 * 1024),
    )(
        place,
        starts,
        levels,
        cos_table,
        sin_table,
        *rotated,
        grad.reshape(2, 2, seq_rows // 2, SHARE),
        *weights,
    )
    return (
        grad_projected.reshape(2 * seq_rows, 3 * SHARE),
        grad_hidden.reshape(2 * seq_rows, D),
    )


BLOCK = 512
NARROW = 512


def narrower(block):
    wide = min(NARROW, block)
    return [slice(at, at + wide) for at in range(0, block, wide)]


def of_two(step, half, body, mine_ref, other_ref):
    @pl.when(step < half)
    def _():
        body(mine_ref)

    @pl.when(step >= half)
    def _():
        body(other_ref)


def lift_kernel(half, gate_ref, limit_ref, unit_ref, mine_ref, other_ref, *others):
    feed_pieces, upstream_pieces = others[:7], others[7:14]
    rectified_ref, activated_ref, grad_ref, feed_all, upstream_all = others[14:19]
    feed_ref, upstream_ref, feed_sem, upstream_sem, out_sem = others[19:]
    step = pl.program_id(0)
    wide = grad_ref.shape[1]
    feed_in = copies_in(feed_pieces, feed_ref, feed_sem)
    upstream_in = copies_in(upstream_pieces, upstream_ref, upstream_sem)
    feed_out = pltpu.make_async_copy(feed_ref, feed_all, out_sem.at[0])
    upstream_out = pltpu.make_async_copy(upstream_ref, upstream_all, out_sem.at[1])

    @pl.when(step == 0)
    def _():
        for copy in feed_in + upstream_in:
            copy.start()
        for copy in feed_in:
            copy.wait()
        feed_out.start()

    def body(up_ref):
        for at in narrower(rectified_ref.shape[1]):
            kept = unit_ref[:, at] < limit_ref[...]
            lifted = dot_plain(feed_ref[...], up_ref[:, at])
            rectified = jnp.where(kept, jnp.maximum(lifted, 0.0), 0.0)
            rectified_ref[:, at] = rectified
            activated_ref[:, at] = (rectified * rectified).astype(bf16)

    of_two(step, half, body, mine_ref, other_ref)

    @pl.when(step == 0)
    def _():
        for copy in upstream_in:
            copy.wait()
        upstream_out.start()

    upstream = upstream_ref[:, pl.ds(pl.multiple_of(step * wide, wide), wide)]
    grad_ref[...] = (gate_ref[...] * upstream.astype(f32)).astype(bf16)

    @pl.when(step == 2 * half - 1)
    def _():
        feed_out.wait()
        upstream_out.wait()


def lift(gate, limit, unit, up_mine, up_other, feed, upstream):
    count, units = gate.shape[0], up_mine.shape[1]
    block = min(BLOCK, units)
    half = units // block
    steps = 2 * half
    wide = D // steps
    return pl.pallas_call(
        functools.partial(lift_kernel, half),
        grid=(steps,),
        in_specs=[
            pl.BlockSpec((count, 1), lambda s: (0, 0)),
            pl.BlockSpec((count, 1), lambda s: (0, 0)),
            pl.BlockSpec((1, block), lambda s: (0, s)),
            pl.BlockSpec((D, block), lambda s: (0, jnp.minimum(s, half - 1))),
            pl.BlockSpec((D, block), lambda s: (0, jnp.maximum(s - half, 0))),
        ]
        + [pl.BlockSpec(memory_space=pl.ANY)] * 14,
        out_specs=[
            pl.BlockSpec((count, block), lambda s: (0, s)),
            pl.BlockSpec((count, block), lambda s: (0, s)),
            pl.BlockSpec((count, wide), lambda s: (0, s)),
            pl.BlockSpec(memory_space=pl.ANY),
            pl.BlockSpec(memory_space=pl.ANY),
        ],
        out_shape=[
            jax.ShapeDtypeStruct((count, 2 * units), f32),
            jax.ShapeDtypeStruct((count, 2 * units), bf16),
            jax.ShapeDtypeStruct((count, D), bf16),
            jax.ShapeDtypeStruct((count, D), bf16),
            jax.ShapeDtypeStruct((count, D), bf16),
        ],
        scratch_shapes=[
            pltpu.VMEM((count, D), bf16),
            pltpu.VMEM((count, D), bf16),
            pltpu.SemaphoreType.DMA((7,)),
            pltpu.SemaphoreType.DMA((7,)),
            pltpu.SemaphoreType.DMA((2,)),
        ],
        compiler_params=pltpu.CompilerParams(vmem_limit_bytes=56 * 1024 * 1024),
    )(gate, limit, unit, up_mine, up_other, *feed, *upstream)


def mixed_back_kernel(weight_ref, *others):
    pieces, (grad_ref, all_ref, whole_ref, sem, out_sem) = others[:7], others[7:]
    copies = copies_in(pieces, whole_ref, sem)
    copy_out = pltpu.make_async_copy(whole_ref, all_ref, out_sem)
    for copy in copies:
        copy.start()
    for copy in copies:
        copy.wait()
    copy_out.start()
    grad_ref[...] = contract_last(whole_ref[...], weight_ref[...]).astype(bf16)
    copy_out.wait()


def mixed_back(weight, pieces):
    count = sum(piece.shape[0] for piece in pieces)
    return pl.pallas_call(
        mixed_back_kernel,
        in_specs=[pl.BlockSpec(memory_space=pltpu.VMEM)]
        + [pl.BlockSpec(memory_space=pl.ANY)] * len(pieces),
        out_specs=[pl.BlockSpec(memory_space=pltpu.VMEM), pl.BlockSpec(memory_space=pl.ANY)],
        out_shape=[
            jax.ShapeDtypeStruct((count, weight.shape[0]), bf16),
            jax.ShapeDtypeStruct((count, D), bf16),
        ],
        scratch_shapes=[
            pltpu.VMEM((count, D), bf16),
            pltpu.SemaphoreType.DMA((len(pieces),)),
            pltpu.SemaphoreType.DMA,
        ],
        compiler_params=pltpu.CompilerParams(vmem_limit_bytes=48 * 1024 * 1024),
    )(weight, *pieces)


def lower_kernel(
    half,
    grad_ref,
    rectified_ref,
    down_mine_ref,
    down_other_ref,
    up_mine_ref,
    up_other_ref,
    lifted_ref,
    input_ref,
    kept_ref,
):
    step = pl.program_id(0)
    count, block = rectified_ref.shape
    units = half * block

    @pl.when(step < 2 * half)
    def _():
        columns = pl.ds(pl.multiple_of(step * block, block), block)

        def body(down_ref):
            for at in narrower(block):
                grad = contract_last(grad_ref[...], down_ref[at, :])
                lifted_ref[:, at] = (grad * 2.0 * rectified_ref[:, at]).astype(bf16)

        of_two(step, half, body, down_mine_ref, down_other_ref)
        kept_ref[:, columns] = lifted_ref[...]

    @pl.when(step >= 2 * half)
    def _():
        for at in narrower(input_ref.shape[1]):
            input_ref[:, at] = (
                contract_last(kept_ref[:, :units], up_mine_ref[at, :])
                + contract_last(kept_ref[:, units:], up_other_ref[at, :])
            ).astype(bf16)


def lower(grad, rectified, down_mine, down_other, up_mine, up_other):
    count, units = grad.shape[0], up_mine.shape[1]
    block = min(BLOCK, units)
    half = units // block
    first, second = 2 * half, D // BLOCK
    once = pl.Buffered(1)
    return pl.pallas_call(
        functools.partial(lower_kernel, half),
        grid=(first + second,),
        in_specs=[
            pl.BlockSpec((count, D), lambda s: (0, 0), pipeline_mode=once),
            pl.BlockSpec((count, block), lambda s: (0, jnp.minimum(s, first - 1))),
            pl.BlockSpec((block, D), lambda s: (jnp.minimum(s, half - 1), 0)),
            pl.BlockSpec((block, D), lambda s: (jnp.clip(s - half, 0, half - 1), 0)),
            pl.BlockSpec((BLOCK, units), lambda s: (jnp.maximum(s - first, 0), 0)),
            pl.BlockSpec((BLOCK, units), lambda s: (jnp.maximum(s - first, 0), 0)),
        ],
        out_specs=[
            pl.BlockSpec((count, block), lambda s: (0, jnp.minimum(s, first - 1))),
            pl.BlockSpec((count, BLOCK), lambda s: (0, jnp.maximum(s - first, 0))),
        ],
        out_shape=[
            jax.ShapeDtypeStruct((count, 2 * units), bf16),
            jax.ShapeDtypeStruct((count, D), bf16),
        ],
        scratch_shapes=[pltpu.VMEM((count, 2 * units), bf16)],
        compiler_params=pltpu.CompilerParams(vmem_limit_bytes=56 * 1024 * 1024),
    )(grad, rectified, down_mine, down_other, up_mine, up_other)


def branch_kernel(activated_ref, upstream_ref, mine_ref, other_ref, branch_ref, part_ref):
    units = mine_ref.shape[0]
    total = None
    for at in narrower(branch_ref.shape[1]):
        branch = dot_plain(activated_ref[:, :units], mine_ref[:, at]) + dot_plain(
            activated_ref[:, units:], other_ref[:, at]
        )
        branch_ref[:, at] = branch.astype(bf16)
        part = jnp.sum(branch * upstream_ref[:, at].astype(f32), axis=1, keepdims=True)
        total = part if total is None else total + part

    @pl.when(pl.program_id(0) == 0)
    def _():
        part_ref[...] = total

    @pl.when(pl.program_id(0) > 0)
    def _():
        part_ref[...] += total


def branch(activated, upstream, down_mine, down_other):
    count, units = activated.shape[0], down_mine.shape[0]
    once = pl.Buffered(1)
    return pl.pallas_call(
        branch_kernel,
        grid=(D // BLOCK,),
        in_specs=[
            pl.BlockSpec((count, 2 * units), lambda s: (0, 0), pipeline_mode=once),
            pl.BlockSpec((count, BLOCK), lambda s: (0, s)),
            pl.BlockSpec((units, BLOCK), lambda s: (0, s)),
            pl.BlockSpec((units, BLOCK), lambda s: (0, s)),
        ],
        out_specs=[
            pl.BlockSpec((count, BLOCK), lambda s: (0, s)),
            pl.BlockSpec((count, 1), lambda s: (0, 0)),
        ],
        out_shape=[
            jax.ShapeDtypeStruct((count, D), bf16),
            jax.ShapeDtypeStruct((count, 1), f32),
        ],
        compiler_params=pltpu.CompilerParams(vmem_limit_bytes=56 * 1024 * 1024),
    )(activated, upstream, down_mine, down_other)


def local(
    planes,
    tokens,
    documents,
    head_level,
    width_level,
    mixer_gain,
    mixer_bias,
    input_weight,
    output_weight,
    mixer_router,
    feed_gain,
    feed_bias,
    up_weight,
    down_weight,
    feed_router,
    cotangent,
):
    rows = tokens.shape[0]
    seq_rows = documents.shape[1]
    weight_rows = input_weight.shape[0]
    unit_rows = down_weight.shape[0]
    at_core = lax.axis_index("c")
    chip = lax.axis_index("x") * 2 + lax.axis_index("y")
    at_plane = chip * 2 + at_core
    quarter = at_plane % (seq_rows // rows)
    place = jnp.stack([quarter, 2 * at_core]).astype(jnp.int32)

    def pieces(values):
        return [values[at : at + rows] for at in range(0, values.shape[0], rows)]

    def both_cores(mine, other):
        return (mine.astype(f32) + flip(other, "c").astype(f32)).astype(bf16)

    levels = jnp.concatenate(
        [head_level.reshape(2, rows // 2), width_level.reshape(2, rows // 2)], axis=1
    )
    levels = levels.astype(f32)
    levels = gather_small(levels)
    plane_docs = jnp.concatenate([documents, flip(documents, "x")], axis=0)
    starts = jnp.sum(
        (plane_docs[:, None, :] < plane_docs[:, :, None]).astype(jnp.int32), axis=2
    ).reshape(2 * seq_rows, 1)
    level_range = jnp.arange(OPTIONS)
    head_counts = jnp.sum((head_level[:, None] == level_range[None, :]).astype(f32), axis=0)
    width_counts = jnp.sum((width_level[:, None] == level_range[None, :]).astype(f32), axis=0)

    output_blocks = [output_weight]
    if planes == 4:
        output_blocks += [
            lax.ppermute(output_weight, "z", [(i, i ^ d) for i in range(planes)])
            for d in range(1, planes)
        ]
    input_first = swap_plane(deal(input_weight, attention_columns()))
    input_first, output_blocks, levels, starts = lax.optimization_barrier(
        (input_first, output_blocks, levels, starts)
    )
    weights = [lax.all_gather(input_first[:, : 3 * HD], "z", axis=0, tiled=True)]
    token_values = tokens.astype(f32)
    mixer_hidden, mixer_normed, mixer_scale = normalize(token_values, mixer_gain, mixer_bias)
    mixer_gate, mixer_probs, mixer_chosen = route(mixer_hidden, mixer_router, head_level)
    mixer_pieces = gather_eight(mixer_hidden.astype(bf16))
    mixer_pieces[1:5], input_second, up_weight, cotangent_sent, weights[0] = (
        lax.optimization_barrier(
            (mixer_pieces[1:5], input_first[:, 3 * HD :], up_weight, cotangent, weights[0])
        )
    )
    weights.append(lax.all_gather(input_second, "z", axis=0, tiled=True))
    output_share = share_heads(output_blocks)
    width_all = levels[:, :, rows // 2 :].reshape(4 * rows)
    limit = (width_all[:, None].astype(jnp.int32) + 1) * (FF // OPTIONS)
    head_all = levels[:, :, : rows // 2].reshape(4, rows)
    head_all = jnp.concatenate([head_all, flip(head_all, "c")], axis=0)
    head_all = head_all.reshape(2, 2, 2 * rows, 1)
    up_first = swap_plane(deal(up_weight, unit_columns(planes, unit_rows)))
    weights[1], up_first = lax.optimization_barrier((weights[1], up_first))
    up_mine = lax.all_gather(up_first, "z", axis=0, tiled=True)
    down_mine = lax.all_gather(after(down_weight, up_first), "z", axis=0, tiled=True)
    upstream_pieces = gather_four(cotangent_sent)

    cos_table, sin_table = rope_tables(jnp.arange(seq_rows).astype(f32))
    attending = functools.partial(attend, place, starts, head_all, cos_table, sin_table)
    rotated_0, mixed_0, mixer_all = attending(weights[0], mixer_pieces, rows, 0)
    weights[1], mixed_0, upstream_pieces[1:5] = lax.optimization_barrier(
        (weights[1], mixed_0, upstream_pieces[1:5])
    )
    rotated_1, mixed_1, _ = attending(weights[1], mixer_pieces, rows, 1)
    mixed = [m.reshape(2, 4 * rows, HD) for m in (mixed_0, mixed_1)]
    mixed_all = jnp.concatenate(
        [m[0] for m in mixed] + [flip(m[1], "c") for m in mixed], axis=1
    )
    mixed_all, upstream_pieces[5:] = lax.optimization_barrier((mixed_all, upstream_pieces[5:]))
    mixer_branch = scatter_four(pieces(dot_plain(mixed_all, output_share).astype(bf16)))
    middle = token_values + mixer_gate[:, None] * mixer_branch
    feed_hidden, feed_normed, feed_scale = normalize(middle, feed_gain, feed_bias)
    feed_gate, feed_probs, feed_chosen = route(feed_hidden, feed_router, width_level)
    upstream = cotangent.astype(f32)

    up_mine, feed_low = lax.optimization_barrier((up_mine, feed_hidden.astype(bf16)))
    up_other = flip(up_mine, "c")
    feed_pieces = gather_four(feed_low)
    gate_all = gather_small(feed_gate.reshape(2, rows // 2)).reshape(4 * rows, 1)
    units = planes * unit_rows
    unit = jnp.arange(units, dtype=jnp.int32)
    unit = jnp.concatenate(
        [
            (unit // unit_rows * GROUP + share) * unit_rows + unit % unit_rows
            for share in (at_plane, at_plane ^ 1)
        ]
    )
    rectified, activated, grad_branch_all, feed_all, upstream_all = lift(
        gate_all, limit, unit[None, :], up_mine, up_other, feed_pieces, upstream_pieces
    )
    down_part_other = contract_first(activated[:, units:], grad_branch_all).astype(bf16)
    down_part = both_cores(
        contract_first(activated[:, :units], grad_branch_all), down_part_other
    )
    down_mine, down_part_other = lax.optimization_barrier((down_mine, down_part_other))
    down_other = flip(down_mine, "c")
    down_sum = lax.psum_scatter(down_part, "z", scatter_dimension=0, tiled=True)
    lifted, input_pieces = lower(
        grad_branch_all, rectified, down_mine, down_other, up_mine, up_other
    )
    activated, input_pieces = lax.optimization_barrier((activated, input_pieces))
    input_pieces = pieces(input_pieces)
    input_sent = scatter_send(input_pieces)
    branch_pieces, gate_part = branch(activated, upstream_all, down_mine, down_other)
    lifted, gate_part, input_sent = lax.optimization_barrier((lifted, gate_part, input_sent))
    grad_feed_gate = sum_small(gate_part.reshape(4, 2, rows // 2)).reshape(rows)
    up_part_other = contract_first(feed_all, lifted[:, units:]).astype(bf16)
    up_part = both_cores(contract_first(feed_all, lifted[:, :units]), up_part_other)
    grad_feed_input = scatter_end(input_pieces, input_sent)

    feed_router_term, grad_feed_routed = route_back(
        grad_feed_gate, feed_probs, feed_chosen, feed_hidden, feed_router
    )
    grad_middle_norm, feed_gain_term, feed_bias_term = normalize_back(
        grad_feed_input + grad_feed_routed, feed_normed, feed_scale, feed_gain
    )
    grad_middle = upstream + grad_middle_norm
    grad_mixer_gate = jnp.sum(mixer_branch * grad_middle, axis=1)
    grad_mixer_branch = (mixer_gate[:, None] * grad_middle).astype(bf16)
    grad_mixer_branch, down_sum, up_part = lax.optimization_barrier(
        (grad_mixer_branch, down_sum, up_part)
    )
    up_sum = lax.psum_scatter(up_part, "z", scatter_dimension=0, tiled=True)
    grad_attended, grad_mixer_all = mixed_back(output_share, gather_four(grad_mixer_branch))
    grad_attended = jnp.concatenate(
        [grad_attended[:, :SHARE], flip(grad_attended[:, SHARE:], "c")], axis=0
    )

    branch_pieces, grad_attended = lax.optimization_barrier((branch_pieces, grad_attended))
    branch_pieces = pieces(branch_pieces)
    branch_sent = scatter_send(branch_pieces)
    output_part = contract_first(mixed_all, grad_mixer_all).astype(bf16)
    grad_projected, mixer_pieces = attend_back(
        place,
        starts,
        head_all,
        cos_table,
        sin_table,
        (rotated_0, rotated_1),
        grad_attended,
        weights,
        rows,
    )
    grad_projected, up_sum, branch_sent = lax.optimization_barrier(
        (grad_projected, up_sum, branch_sent)
    )
    feed_branch = scatter_end(branch_pieces, branch_sent)
    input_part = contract_first(mixer_all, grad_projected).astype(bf16)
    input_sum = lax.psum_scatter(input_part, "z", scatter_dimension=0, tiled=True)
    mixer_pieces, feed_branch = lax.optimization_barrier(
        (add_cores(pieces(mixer_pieces)), feed_branch)
    )
    outputs = (middle + feed_gate[:, None] * feed_branch).astype(bf16)
    grad_mixer_input = scatter_four(mixer_pieces)
    input_sum, output_part = lax.optimization_barrier((input_sum, output_part))
    grad_output_weight = sum_heads(output_part, planes, weight_rows).astype(f32)
    grad_mixer_input, up_sum = lax.optimization_barrier((grad_mixer_input, up_sum))
    up_back = swap_plane(up_sum)

    mixer_router_term, grad_mixer_routed = route_back(
        grad_mixer_gate, mixer_probs, mixer_chosen, mixer_hidden, mixer_router
    )
    grad_token_norm, mixer_gain_term, mixer_bias_term = normalize_back(
        grad_mixer_input + grad_mixer_routed, mixer_normed, mixer_scale, mixer_gain
    )
    grad_tokens = grad_middle + grad_token_norm
    counts = jnp.pad(jnp.concatenate([head_counts, width_counts]), (0, D - 2 * OPTIONS))
    rows_of = [mixer_gain_term, mixer_bias_term, feed_gain_term, feed_bias_term, counts]
    sums, input_back = sum_everywhere(
        jnp.concatenate([jnp.stack(rows_of), mixer_router_term, feed_router_term], axis=0),
        planes,
        swap_plane(input_sum),
    )
    grad_down_weight = down_sum.astype(f32)
    grad_up_weight = undeal(up_back, unit_columns(planes, unit_rows))
    grad_input_weight = undeal(input_back, attention_columns())
    return (
        outputs,
        grad_tokens,
        sums[0],
        sums[1],
        grad_input_weight,
        grad_output_weight,
        sums[5:9].T,
        sums[2],
        sums[3],
        grad_up_weight,
        grad_down_weight,
        sums[9:13].T,
        sums[4, : 2 * OPTIONS].reshape(2, OPTIONS),
    )


def solution(mesh):
    wide, narrow = mesh.shape["wide"], mesh.shape["narrow"]
    planes = wide // 2
    inner = Mesh(mesh.devices.reshape(planes, 2, narrow // 2, 2), ALL)
    rowwise = P(ALL, None)
    in_specs = (
        rowwise,
        P(("z", "x"), None),
        P(ALL),
        P(ALL),
        P(),
        P(),
        rowwise,
        rowwise,
        P(),
        P(),
        P(),
        rowwise,
        rowwise,
        P(),
        rowwise,
    )
    out_specs = (
        rowwise,
        rowwise,
        P(),
        P(),
        rowwise,
        rowwise,
        P(),
        P(),
        P(),
        rowwise,
        rowwise,
        P(),
        P(),
    )
    return jax.shard_map(
        functools.partial(local, planes),
        mesh=inner,
        in_specs=in_specs,
        out_specs=out_specs,
        check_vma=False,
    )
```
